256 devices in a mesh: rep: 32 (over z, x_hi, core), fsdp: 8 (over x_lo, y).
Axes of the slice: x: 4 (x_hi: 2, x_lo: 2; x = x_hi * 2 + x_lo), y: 4, z: 8, core: 2. Of those that a mesh axis runs over, the one named last changes fastest.
Arguments:
- tokens: bfloat16 [65536, 5120], P(('rep', 'fsdp')), may hold values from -6 to 6
- cotangent: bfloat16 [65536, 5120], P(('rep', 'fsdp')), may hold values from -0.119628906 to 0.119628906
- token_row: int32 [65536], P(('rep', 'fsdp')), may hold values from 0 to 43
- token_col: int32 [65536], P(('rep', 'fsdp')), may hold values from 0 to 79
- token_frame: int32 [65536], P(('rep', 'fsdp')), may hold values from 0 to 23
- token_camera: int32 [65536], P(('rep', 'fsdp')), may hold values from 0 to 3
- pixel_depth: float32 [128, 65536], P(None, ('rep', 'fsdp')), may hold values from 0.5 to 4
- cam_poses: float32 [32, 12, 96], P('rep'), may hold values from -3 to 3, as said below
- cam_weight: bfloat16 [32, 768, 5120], P('rep', 'fsdp'), may hold values from -0.21875 to 0.21875
- gain: float32 [32, 5120], P('rep'), may hold values from 0.1 to 1.9
- frag_stack: bfloat16 [32, 6, 5120, 256], P('rep', None, 'fsdp'), may hold values from -6 to 6
- frag_block: int32 [6], replicated, may hold values from 0 to 5, each once
- global_frag: float32 [5120, 256], P('fsdp'), may hold values from -6 to 6
- momentum: float32 [5120, 256], P('fsdp'), may hold values from -3 to 3
Outputs:
- cam_grad: bfloat16 [32, 768, 5120], P('rep', 'fsdp')
- gain_grad: float32 [32, 5120], P('rep', 'fsdp')
- new_global: float32 [5120, 256], P('fsdp')
- new_momentum: float32 [5120, 256], P('fsdp')
- merged_frag: bfloat16 [32, 5120, 256], P('rep', 'fsdp')
The draws below stay inside these ranges and needn't reach their ends.
Inputs may be any that keep to these rules, and one draw needn't show every extreme that they name: `frag_block`: each held block appears once; entry 0 is the block that syncs now. `cam_poses`: for every pose, entries 0 to 8 form a rotation matrix in row-major order; entries 9 to 11 are the camera position.
All inputs are finite; a program needn't handle non-finite values.
Results may differ from the reference program's by a relative error of at most 0.014.
Values may be sent and summed in bfloat16 or wider, within the bound.
A program may use at most 128 MiB of HBM per device.

```python
import math
import jax
import jax.numpy as jnp
from jax import lax

D = 5120
R = 256
PIX = 128
NBL = 6
NCAM = 4
NFRAME = 24
GH = 44
GW = 80
PIN = 768
POSES = 96
TOKENS = 65536
N_REP = 32


def draw_cam_poses(key, part):
    key = jax.random.fold_in(key, 7)
    key_angle, key_place = jax.random.split(key)
    angles = jax.random.uniform(key_angle, (3, N_REP, POSES), jnp.float32, -math.pi, math.pi)
    place = jax.random.uniform(key_place, (3, N_REP, POSES), jnp.float32, -3.0, 3.0)
    cos_a = jnp.cos(angles[0])
    sin_a = jnp.sin(angles[0])
    cos_b = jnp.cos(angles[1])
    sin_b = jnp.sin(angles[1])
    cos_c = jnp.cos(angles[2])
    sin_c = jnp.sin(angles[2])
    entries = [cos_a * cos_b, cos_a * sin_b * sin_c - sin_a * cos_c, cos_a * sin_b * cos_c + sin_a * sin_c, sin_a * cos_b, sin_a * sin_b * sin_c + cos_a * cos_c, sin_a * sin_b * cos_c - cos_a * sin_c, -sin_b, cos_b * sin_c, cos_b * cos_c, place[0], place[1], place[2]]
    return jnp.stack(entries, axis=1).astype(jnp.float32)


def place_ends(drawn, rng, least, high):
    spot = [jax.random.randint(jax.random.fold_in(rng, axis), (), 0, length) for axis, length in enumerate(drawn.shape)]
    longest = drawn.shape.index(max(drawn.shape))
    neighbour = spot[:longest] + [(spot[longest] + 1) % drawn.shape[longest]] + spot[longest + 1:]
    return drawn.at[tuple(spot)].set(least).at[tuple(neighbour)].set(high)


def shard_levels(rng, extent, shards, smallest, largest):
    loudness, own = 1.0, jax.random.fold_in(rng, 6)
    for position, blocks in shards:
        draws = jnp.exp(jax.random.uniform(jax.random.fold_in(own, position), (blocks,), jnp.float32, smallest / len(shards), largest / len(shards)))
        loudness = loudness * jnp.repeat(draws, extent[position] // blocks).reshape([-1 if axis == position else 1 for axis in range(len(extent))])
    return loudness


def centred(key, dims, deviation, bound, pieces=(), held_as=jnp.bfloat16):
    array = deviation * jax.random.normal(key, dims, jnp.float32)
    if pieces:
        array = array * shard_levels(key, dims, pieces, -0.22, 0.18)
    return jnp.clip(array, -bound, bound).astype(held_as)


def setup_inputs(seed: int = 0) -> dict:
    keys = jax.random.split(jax.random.key(seed), 15)
    return {
        "tokens": centred(keys[0], (TOKENS, D), 1.0, 6.0, ((0, 256),)),
        "cotangent": centred(keys[1], (TOKENS, D), 0.02, 0.119628906, ((0, 256),)),
        "token_row": place_ends(jax.random.randint(keys[2], (TOKENS,), 0, GH), jax.random.fold_in(keys[2], 1), 0, GH - 1).astype(jnp.int32),
        "token_col": place_ends(jax.random.randint(keys[3], (TOKENS,), 0, GW), jax.random.fold_in(keys[3], 1), 0, GW - 1).astype(jnp.int32),
        "token_frame": place_ends(jax.random.randint(keys[4], (TOKENS,), 0, NFRAME), jax.random.fold_in(keys[4], 1), 0, NFRAME - 1).astype(jnp.int32),
        "token_camera": place_ends(jax.random.randint(keys[5], (TOKENS,), 0, NCAM), jax.random.fold_in(keys[5], 1), 0, NCAM - 1).astype(jnp.int32),
        "pixel_depth": jnp.clip(jnp.exp(math.log(4.0) - 2.0794415 * jax.random.uniform(keys[6], (PIX, TOKENS), jnp.float32) ** shard_levels(keys[6], (PIX, TOKENS), ((1, 256),), -0.2, 0.2)), 0.5, 4.0),
        "cam_poses": draw_cam_poses(jax.random.fold_in(keys[14], 71), 0),
        "cam_weight": centred(keys[8], (N_REP, PIN, D), PIN ** -0.5, 0.21875, ((0, 32), (1, 8))),
        "gain": jnp.clip(1.0 + 0.18 * jax.random.normal(keys[9], (N_REP, D), jnp.float32), 0.1, 1.9),
        "frag_stack": centred(keys[10], (N_REP, NBL, D, R), 1.0, 6.0, ((0, 32), (2, 8))),
        "frag_block": jax.random.permutation(keys[11], NBL).astype(jnp.int32),
        "global_frag": centred(keys[12], (D, R), 1.0, 6.0, ((0, 8),), jnp.float32),
        "momentum": centred(keys[13], (D, R), 0.5, 3.0, ((0, 8),), jnp.float32),
    }


EPS = 1e-06
MOMENTUM_RATE = 0.9
OUTER_RATE = 0.7
MIX_RATE = 0.5

def ray_features(token_row, token_col, token_frame, token_camera, pixel_depth, poses):
    pose_index = (token_camera * NFRAME + token_frame).astype(jnp.int32)
    per_token = jnp.take(poses, pose_index, axis=1)
    pixel = jnp.arange(PIX, dtype=jnp.int32)[:, None]
    sub_rows = PIX // 16
    across = (token_col[None, :] * 16 + pixel % 16).astype(jnp.float32)
    down = (token_row[None, :] * sub_rows + pixel // 16).astype(jnp.float32)
    horiz = (across + 0.5) / (GW * 16) * 2.0 - 1.0
    vert = (down + 0.5) / (GH * sub_rows) * 2.0 - 1.0
    dir_x = per_token[0][None, :] * horiz + per_token[1][None, :] * vert + per_token[2][None, :]
    dir_y = per_token[3][None, :] * horiz + per_token[4][None, :] * vert + per_token[5][None, :]
    dir_z = per_token[6][None, :] * horiz + per_token[7][None, :] * vert + per_token[8][None, :]
    length = jnp.sqrt(dir_x * dir_x + dir_y * dir_y + dir_z * dir_z)
    unit_x = dir_x / length
    unit_y = dir_y / length
    unit_z = dir_z / length
    near_x = unit_x / pixel_depth
    near_y = unit_y / pixel_depth
    near_z = unit_z / pixel_depth
    point_x = per_token[9][None, :] + pixel_depth * unit_x
    point_y = per_token[10][None, :] + pixel_depth * unit_y
    point_z = per_token[11][None, :] + pixel_depth * unit_z
    stacked = jnp.stack([near_x, near_y, near_z, point_x, point_y, point_z])
    return stacked.reshape(6 * PIX, token_row.shape[0]).astype(jnp.bfloat16)

def replica_block(items):
    tokens, cotangent, token_row, token_col, token_frame, token_camera, depth, poses, weight, gain = items
    rays = ray_features(token_row, token_col, token_frame, token_camera, depth, poses)
    lifted = jnp.dot(rays.T, weight, preferred_element_type=jnp.float32)
    hidden = tokens.astype(jnp.float32) + lifted
    scale = lax.rsqrt(lax.optimization_barrier(jnp.mean(hidden * hidden, axis=1, keepdims=True)) + EPS)
    normed = hidden * scale
    upstream = cotangent.astype(jnp.float32)
    gain_grad = lax.optimization_barrier(jnp.sum(upstream * normed, axis=0))
    pushed = upstream * gain[None, :]
    slope = (scale * (pushed - normed * lax.optimization_barrier(jnp.mean(pushed * normed, axis=1, keepdims=True)))).astype(jnp.bfloat16)
    weight_grad = jnp.dot(rays, slope, preferred_element_type=jnp.float32).astype(jnp.bfloat16)
    return (weight_grad, gain_grad)

def reference(tokens, cotangent, token_row, token_col, token_frame, token_camera, pixel_depth, cam_poses, cam_weight, gain, frag_stack, frag_block, global_frag, momentum):
    per_rep = tokens.shape[0] // N_REP
    depth_rep = jnp.transpose(pixel_depth.reshape(PIX, N_REP, per_rep), (1, 0, 2))
    items = (tokens.reshape(N_REP, per_rep, D), cotangent.reshape(N_REP, per_rep, D), token_row.reshape(N_REP, per_rep), token_col.reshape(N_REP, per_rep), token_frame.reshape(N_REP, per_rep), token_camera.reshape(N_REP, per_rep), depth_rep, cam_poses, cam_weight, gain)
    cam_grad, gain_grad = lax.map(replica_block, items)
    chosen = lax.dynamic_index_in_dim(frag_stack, frag_block[0], 1, keepdims=False).astype(jnp.float32)
    average = lax.optimization_barrier(jnp.sum(chosen, axis=0)) / N_REP
    delta = global_frag - average
    new_momentum = MOMENTUM_RATE * momentum + delta
    new_global = global_frag - OUTER_RATE * (MOMENTUM_RATE * new_momentum + delta)
    merged_frag = (MIX_RATE * chosen + (1.0 - MIX_RATE) * new_global[None]).astype(jnp.bfloat16)
    return (cam_grad, gain_grad, new_global, new_momentum, merged_frag)
```

```python
import jax
import jax.numpy as jnp
from jax import lax
from jax.experimental import pallas as pl
from jax.experimental.pallas import tpu as pltpu
from jax.sharding import PartitionSpec as P

D = 5120
PIX = 128
NFRAME = 24
GH = 44
GW = 80
PIN = 768
POSES = 96
N_REP = 32
SHARE = 8
DS = D // SHARE
ROWS = PIN // SHARE
TOK = 256
CHUNKS = 4
TC = TOK // CHUNKS
CT = SHARE * TC
FR = 640
FP = 80
MSG = TOK + 16

EPS = 1e-06
MOMENTUM_RATE = 0.9
OUTER_RATE = 0.7
MIX_RATE = 0.5

MESH = pl.DeviceIdType.MESH
F32 = jnp.float32
BF16 = jnp.bfloat16


def spread(row):
    return jnp.broadcast_to(row, (128, 128)).T


def kernel(
    tok, cot, trow, tcol, tfr, tcam, depth, poses, weight, gain, frag, block, glob, mom,
    grad_out, gain_out, glob_out, mom_out, merged_out,
    tokv, cotv, wv, msg, depthv, idxv, posev, gainv, table_hi, table_lo,
    rays_t, rays, hid, slope, acc, grad, gacc, stat,
    fragv, chosen, fpart, fsum, fother, avg, globv, momv, mergedv,
    lsem, main_s, main_r, w_s, w_r, msg_s, msg_r, st_s, st_r, g_s, g_r,
    f_s, f_r, h_s, h_r, b_s, b_r,
):
    rep, me = lax.axis_index("rep"), lax.axis_index("fsdp")
    z, xh, core = rep // 4, lax.rem(rep // 2, 2), lax.rem(rep, 2)

    def flip(a, b, bits):
        out = a
        for i in range(bits):
            if b >> i & 1:
                bit = lax.rem(a // (1 << i), 2)
                out = out + (1 << i) * (1 - 2 * bit)
        return out

    peer = [flip(me, s, 3) for s in range(SHARE)]
    mate = [(flip(z, s >> 1, 3), flip(core, s & 1, 1)) for s in range(16)]

    def mate_rep(s):
        return mate[s][0] * 4 + xh * 2 + mate[s][1]

    across = z * 4 + (1 - xh) * 2 + core

    local = [
        pltpu.make_async_copy(depth, depthv, lsem.at[0]),
        pltpu.make_async_copy(trow, idxv.at[0], lsem.at[1]),
        pltpu.make_async_copy(tcol, idxv.at[1], lsem.at[2]),
        pltpu.make_async_copy(tfr, idxv.at[2], lsem.at[3]),
        pltpu.make_async_copy(tcam, idxv.at[3], lsem.at[4]),
        pltpu.make_async_copy(poses, posev, lsem.at[5]),
        pltpu.make_async_copy(gain.at[:, pl.ds(me * DS, DS)], gainv, lsem.at[6]),
        pltpu.make_async_copy(frag.at[0], fragv, lsem.at[7]),
        pltpu.make_async_copy(glob, globv, lsem.at[8]),
        pltpu.make_async_copy(mom, momv, lsem.at[9]),
        pltpu.make_async_copy(
            weight.at[0, :, pl.ds(me * DS, DS)], wv.at[pl.ds(me * ROWS, ROWS)], lsem.at[10]
        ),
    ]
    for copy in local:
        copy.start()

    barrier = pltpu.get_barrier_semaphore()
    for s in range(1, SHARE):
        pl.semaphore_signal(barrier, inc=1, device_id=(rep, peer[s]), device_id_type=MESH)
    for s in range(1, 16):
        pl.semaphore_signal(barrier, inc=1, device_id=(mate_rep(s), me), device_id_type=MESH)
    pl.semaphore_signal(barrier, inc=1, device_id=(across, me), device_id_type=MESH)
    pl.semaphore_wait(barrier, SHARE - 1 + 15 + 1)

    def remote(src, dst, send, recv, device):
        return pltpu.make_async_remote_copy(
            src_ref=src, dst_ref=dst, send_sem=send, recv_sem=recv, device_id=device, device_id_type=MESH
        )

    w_copies = [
        remote(
            weight.at[0, :, pl.ds(peer[s] * DS, DS)],
            wv.at[pl.ds(me * ROWS, ROWS)],
            w_s.at[s], w_r.at[s], (rep, peer[s]),
        )
        for s in range(1, SHARE)
    ]
    for copy in w_copies:
        copy.start()

    for i in range(5):
        local[i].wait()
    msg[me, pl.ds(0, TOK), :] = depthv[...].T.astype(BF16)
    spot = jnp.concatenate(
        [
            (idxv[3] * NFRAME + idxv[2]).astype(F32),
            idxv[1].astype(F32),
            idxv[0].astype(F32),
            jnp.zeros((10, 128), F32),
        ],
        axis=0,
    )
    msg[me, pl.ds(TOK, 16), :] = spot.astype(BF16)
    msg_copies = [
        remote(msg.at[me], msg.at[me], msg_s.at[s], msg_r.at[s], (rep, peer[s]))
        for s in range(1, SHARE)
    ]
    for copy in msg_copies:
        copy.start()

    def main_copies(c):
        out = []
        for k, (src, dst) in enumerate(((tok, tokv), (cot, cotv))):
            for s in range(SHARE):
                source = src.at[pl.ds(c * TC, TC), pl.ds(peer[s] * DS, DS)]
                target = dst.at[c, pl.ds(pl.multiple_of(me * TC, TC), TC)]
                if s == 0:
                    out.append(pltpu.make_async_copy(source, target, main_r.at[c, k, 0]))
                else:
                    out.append(
                        remote(source, target, main_s.at[c, k, s], main_r.at[c, k, s], (rep, peer[s]))
                    )
        return out

    mains = [main_copies(c) for c in range(CHUNKS)]
    for c in range(2):
        for copy in mains[c]:
            copy.start()

    local[7].wait()
    chosen[...] = fragv[block[0]]
    f_copies = [
        remote(
            chosen.at[pl.ds(mate[s][0] * FP, FP), pl.ds(mate[s][1] * 128, 128)],
            fpart.at[s],
            f_s.at[s], f_r.at[s], (mate_rep(s), me),
        )
        for s in range(1, 16)
    ]
    for copy in f_copies:
        copy.start()

    local[5].wait()
    pixel = lax.broadcasted_iota(jnp.int32, (1, PIX), 1)
    sub_rows = PIX // 16
    horiz = (lax.rem(pixel, 16).astype(F32) + 0.5) / (GW * 16) * 2.0 - 1.0
    vert = ((pixel // 16).astype(F32) + 0.5) / (GH * sub_rows) * 2.0 - 1.0
    table_hi[...] = jnp.zeros_like(table_hi)
    table_lo[...] = jnp.zeros_like(table_lo)

    def put(part, channel, value):
        high = value.astype(BF16)
        where = (pl.ds(part * 128, POSES), pl.ds(channel * PIX, PIX))
        table_hi[where] = high
        table_lo[where] = (value - high.astype(F32)).astype(BF16)

    def entry(k):
        return jnp.broadcast_to(posev[k], (128, POSES)).T

    for ch in range(3):
        first, second, third = entry(3 * ch), entry(3 * ch + 1), entry(3 * ch + 2)
        put(0, ch, first * horiz + second * vert + third)
        put(1, ch, first * (2.0 / GW))
        put(2, ch, second * (2.0 / GH))
        put(0, 3 + ch, entry(9 + ch))

    for copy in msg_copies:
        copy.wait_recv()

    lane = lax.broadcasted_iota(jnp.int32, (128, 128), 1).astype(F32)

    def ray_block(s, _):
        spots = msg[s, pl.ds(TOK, 16), :].astype(F32)
        for half in range(2):
            hot = jnp.where(spread(spots[half : half + 1]) == lane, 1.0, 0.0)
            left = jnp.concatenate(
                [
                    hot,
                    hot * spread(spots[2 + half : 3 + half]),
                    hot * spread(spots[4 + half : 5 + half]),
                ],
                axis=1,
            ).astype(BF16)
            geo = jnp.dot(left, table_hi[...], preferred_element_type=F32) + jnp.dot(
                left, table_lo[...], preferred_element_type=F32
            )
            d = [geo[:, i * PIX : (i + 1) * PIX] for i in range(6)]
            far = msg[s, pl.ds(half * 128, 128), :].astype(F32)
            inv = lax.rsqrt(d[0] * d[0] + d[1] * d[1] + d[2] * d[2])
            near = inv / far
            long = inv * far
            for i in range(6):
                value = (d[i] * near if i < 3 else d[i] + d[i - 3] * long).astype(BF16)
                for q in range(128 // TC):
                    c = half * (128 // TC) + q
                    start = pl.multiple_of(s * TC, TC)
                    rays_t[c, pl.ds(start, TC), pl.ds(i * PIX, PIX)] = value[q * TC : (q + 1) * TC]
        return 0

    lax.fori_loop(0, SHARE, ray_block, 0)

    def turn(k, _):
        c, b = k // (CT // 128), lax.rem(k, CT // 128)
        start = pl.multiple_of(b * 128, 128)
        rays[c, :, pl.ds(start, 128)] = rays_t[c, pl.ds(start, 128), :].T
        return 0

    lax.fori_loop(0, CHUNKS * (CT // 128), turn, 0)

    for copy in f_copies:
        copy.wait_recv()
    total = chosen[pl.ds(pl.multiple_of(z * FP, 16), FP), pl.ds(pl.multiple_of(core * 128, 128), 128)].astype(F32)
    for s in range(1, 16):
        total = total + fpart[s].astype(F32)
    fsum[...] = total
    h_copy = remote(fsum, fother, h_s.at[0], h_r.at[0], (across, me))
    h_copy.start()

    for copy in w_copies:
        copy.wait_recv()
    local[6].wait()
    local[10].wait()
    gain_row = gainv[...]
    gacc[...] = jnp.zeros_like(gacc)

    b_copies = []

    def forward(c):
        def body(b, _):
            at = pl.ds(pl.multiple_of(b * 128, 128), 128)
            lifted = jnp.dot(rays_t[c, at, :], wv[...], preferred_element_type=F32)
            hidden = tokv[c, at, :].astype(F32) + lifted
            hid[c, at, :] = hidden
            square = hidden * hidden
            cross = hidden * (cotv[c, at, :].astype(F32) * gain_row)
            q1, q2 = square[:, :128], cross[:, :128]
            for k in range(1, DS // 128):
                q1 = q1 + square[:, k * 128 : (k + 1) * 128]
                q2 = q2 + cross[:, k * 128 : (k + 1) * 128]
            stat[c, 0, pl.ds(b, 1), :] = jnp.sum(q1.T, axis=0, keepdims=True)
            stat[c, 0, pl.ds(b + CT // 128, 1), :] = jnp.sum(q2.T, axis=0, keepdims=True)
            return 0

        lax.fori_loop(0, CT // 128, body, 0)

    def stat_copies(c):
        return [
            remote(stat.at[c, 0], stat.at[c, s], st_s.at[c, s], st_r.at[c, s], (rep, peer[s]))
            for s in range(1, SHARE)
        ]

    def backward(c):
        both = stat[c, 0]
        for s in range(1, SHARE):
            both = both + stat[c, s]
        scale = lax.rsqrt(both[: CT // 128] / D + EPS)
        pull = scale * scale * scale * (both[CT // 128 :] / D)
        for b in range(CT // 128):
            wide = spread(scale[b : b + 1])
            wide_pull = spread(pull[b : b + 1])
            at = pl.ds(b * 128, 128)
            for k in range(DS // 128):
                cols = pl.ds(k * 128, 128)
                hidden = hid[c, at, cols]
                up = cotv[c, at, cols].astype(F32) * wide
                slope[at, cols] = (up * gainv[:, cols] - wide_pull * hidden).astype(BF16)
                prod = up * hidden
                part = prod[0:8]
                for i in range(1, 16):
                    part = part + prod[i * 8 : (i + 1) * 8]
                gacc[:, cols] += part

    def spend(c):
        def body(i, _):
            at = pl.ds(pl.multiple_of(i * 192, 192), 192)
            new = jnp.dot(rays[c, at, :], slope[...], preferred_element_type=F32)
            if c == 0:
                acc[at, :] = new
            else:
                acc[at, :] += new
            return 0

        lax.fori_loop(0, PIN // 192, body, 0)

    stats = [stat_copies(c) for c in range(CHUNKS)]
    for c in range(CHUNKS):
        for copy in mains[c]:
            copy.wait_recv() if copy.is_remote else copy.wait()
        if c + 2 < CHUNKS:
            for copy in mains[c]:
                if copy.is_remote:
                    copy.wait_send()
            for copy in mains[c + 2]:
                copy.start()
        forward(c)
        for copy in stats[c]:
            copy.start()
        if c == 0:
            h_copy.wait_recv()
            avg[pl.ds(pl.multiple_of(z * FP, 16), FP), pl.ds(pl.multiple_of(core * 128, 128), 128)] = (
                (fsum[...] + fother[...]) * (1.0 / N_REP)
            ).astype(BF16)
            own = avg.at[pl.ds(z * FP, FP), pl.ds(core * 128, 128)]
            b_copies += [
                remote(own, own, b_s.at[s], b_r.at[s], (mate_rep(s), me)) for s in range(1, 16)
            ]
            for copy in b_copies:
                copy.start()
        if c == 2:
            for copy in b_copies:
                copy.wait_recv()
            local[8].wait()
            local[9].wait()

            def nesterov(i, _):
                at = pl.ds(pl.multiple_of(i * 64, 64), 64)
                delta = globv[at, :] - avg[at, :].astype(F32)
                moment = MOMENTUM_RATE * momv[at, :] + delta
                new = globv[at, :] - OUTER_RATE * (MOMENTUM_RATE * moment + delta)
                momv[at, :] = moment
                globv[at, :] = new
                mergedv[at, :] = (
                    MIX_RATE * chosen[at, :].astype(F32) + (1.0 - MIX_RATE) * new
                ).astype(BF16)
                return 0

            lax.fori_loop(0, FR // 64, nesterov, 0)
            outs = [
                pltpu.make_async_copy(globv, glob_out, lsem.at[8]),
                pltpu.make_async_copy(momv, mom_out, lsem.at[9]),
                pltpu.make_async_copy(mergedv, merged_out.at[0], lsem.at[7]),
            ]
            for copy in outs:
                copy.start()
        if c > 0:
            for copy in stats[c - 1]:
                copy.wait_recv()
            backward(c - 1)
            spend(c - 1)
    last = CHUNKS - 1
    for copy in stats[last]:
        copy.wait_recv()
    backward(last)

    g_copies = []
    for k in (1, 2, 3, 0):
        pair = flip(me // 2, k, 2)
        at = pl.ds(pl.multiple_of(pair * 192, 192), 192)
        grad[at, :] = (
            acc[at, :] + jnp.dot(rays[last, at, :], slope[...], preferred_element_type=F32)
        ).astype(BF16)
        for s in (2 * k, 2 * k + 1):
            source = grad.at[pl.ds(peer[s] * ROWS, ROWS)]
            target = grad_out.at[0, :, pl.ds(me * DS, DS)]
            if s == 0:
                mine = pltpu.make_async_copy(source, target, lsem.at[10])
                mine.start()
            else:
                copy = remote(source, target, g_s.at[s], g_r.at[s], (rep, peer[s]))
                copy.start()
                g_copies.append(copy)
    gainv[...] = jnp.sum(gacc[...], axis=0, keepdims=True)
    gain_copy = pltpu.make_async_copy(gainv, gain_out, lsem.at[6])
    gain_copy.start()

    for copy in outs:
        copy.wait()
    gain_copy.wait()
    mine.wait()
    for copy in w_copies + msg_copies + f_copies + [h_copy] + b_copies:
        copy.wait_send()
    for c in range(CHUNKS):
        if c + 2 >= CHUNKS:
            for copy in mains[c]:
                if copy.is_remote:
                    copy.wait_send()
        for copy in stats[c]:
            copy.wait_send()
    for copy in g_copies:
        copy.wait()


def shards(
    tokens, cotangent, token_row, token_col, token_frame, token_camera, pixel_depth,
    cam_poses, cam_weight, gain, frag_stack, frag_block, global_frag, momentum,
):
    dma = pltpu.SemaphoreType.DMA
    hbm = pl.BlockSpec(memory_space=pltpu.HBM)
    places = [a.reshape(2, 128) for a in (token_row, token_col, token_frame, token_camera)]
    return pl.pallas_call(
        kernel,
        name="step",
        out_shape=(
            jax.ShapeDtypeStruct((1, ROWS, D), BF16),
            jax.ShapeDtypeStruct((1, DS), F32),
            jax.ShapeDtypeStruct((FR, 256), F32),
            jax.ShapeDtypeStruct((FR, 256), F32),
            jax.ShapeDtypeStruct((1, FR, 256), BF16),
        ),
        in_specs=[hbm] * 11 + [pl.BlockSpec(memory_space=pltpu.SMEM)] + [hbm] * 2,
        out_specs=(hbm,) * 5,
        scratch_shapes=[
            pltpu.VMEM((CHUNKS, CT, DS), BF16),
            pltpu.VMEM((CHUNKS, CT, DS), BF16),
            pltpu.VMEM((PIN, DS), BF16),
            pltpu.VMEM((SHARE, MSG, 128), BF16),
            pltpu.VMEM((PIX, TOK), F32),
            pltpu.VMEM((4, 2, 128), jnp.int32),
            pltpu.VMEM((12, 1, POSES), F32),
            pltpu.VMEM((1, DS), F32),
            pltpu.VMEM((384, PIN), BF16),
            pltpu.VMEM((384, PIN), BF16),
            pltpu.VMEM((CHUNKS, CT, PIN), BF16),
            pltpu.VMEM((CHUNKS, PIN, CT), BF16),
            pltpu.VMEM((CHUNKS, CT, DS), F32),
            pltpu.VMEM((CT, DS), BF16),
            pltpu.VMEM((PIN, DS), F32),
            pltpu.VMEM((PIN, DS), BF16),
            pltpu.VMEM((8, DS), F32),
            pltpu.VMEM((CHUNKS, SHARE, 2 * CT // 128, 128), F32),
            pltpu.VMEM((6, FR, 256), BF16),
            pltpu.VMEM((FR, 256), BF16),
            pltpu.VMEM((16, FP, 128), BF16),
            pltpu.VMEM((FP, 128), F32),
            pltpu.VMEM((FP, 128), F32),
            pltpu.VMEM((FR, 256), BF16),
            pltpu.VMEM((FR, 256), F32),
            pltpu.VMEM((FR, 256), F32),
            pltpu.VMEM((FR, 256), BF16),
            dma((11,)),
            dma((CHUNKS, 2, SHARE)), dma((CHUNKS, 2, SHARE)),
            dma((SHARE,)), dma((SHARE,)),
            dma((SHARE,)), dma((SHARE,)),
            dma((CHUNKS, SHARE)), dma((CHUNKS, SHARE)),
            dma((SHARE,)), dma((SHARE,)),
            dma((16,)), dma((16,)),
            dma((1,)), dma((1,)),
            dma((16,)), dma((16,)),
        ],
        compiler_params=pltpu.CompilerParams(
            collective_id=0, has_side_effects=True, vmem_limit_bytes=60 << 20
        ),
        cost_estimate=pl.CostEstimate(flops=6 << 30, bytes_accessed=20 << 20, transcendentals=0),
    )(
        tokens, cotangent, *places, pixel_depth, cam_poses.transpose(1, 0, 2), cam_weight, gain,
        frag_stack, frag_block, global_frag, momentum,
    )


def solution(mesh):
    placed = (
        P(("rep", "fsdp"), None),
        P(("rep", "fsdp"), None),
        P(("rep", "fsdp")),
        P(("rep", "fsdp")),
        P(("rep", "fsdp")),
        P(("rep", "fsdp")),
        P(None, ("rep", "fsdp")),
        P("rep", None, None),
        P("rep", "fsdp", None),
        P("rep", None),
        P("rep", None, "fsdp", None),
        P(),
        P("fsdp", None),
        P("fsdp", None),
    )
    return jax.shard_map(
        shards,
        mesh=mesh,
        in_specs=placed,
        out_specs=(
            P("rep", "fsdp", None),
            P("rep", "fsdp"),
            P("fsdp", None),
            P("fsdp", None),
            P("rep", "fsdp", None),
        ),
        check_vma=False,
    )
```

```python
import jax
import jax.numpy as jnp
from jax import lax
from jax.experimental import pallas as pl
from jax.experimental.pallas import tpu as pltpu
from jax.sharding import PartitionSpec as P

D = 5120
PIX = 128
NFRAME = 24
GH = 44
GW = 80
PIN = 768
POSES = 96
N_REP = 32
SHARE = 8
DS = D // SHARE
ROWS = PIN // SHARE
TOK = 256
CHUNKS = 4
TC = TOK // CHUNKS
CT = SHARE * TC
FR = 640
FP = 80
MSG = TOK + 16

EPS = 1e-06
MOMENTUM_RATE = 0.9
OUTER_RATE = 0.7
MIX_RATE = 0.5

MESH = pl.DeviceIdType.MESH
F32 = jnp.float32
BF16 = jnp.bfloat16


def spread(row):
    return jnp.broadcast_to(row, (128, 128)).T


def kernel(
    tok, cot, trow, tcol, tfr, tcam, depth, poses, weight, gain, frag, block, glob, mom,
    grad_out, gain_out, glob_out, mom_out, merged_out,
    tokv, cotv, wv, msg, depthv, idxv, posev, gainv, table_hi, table_lo,
    rays_t, rays, hid, slope, acc, grad, gacc, stat,
    fragv, chosen, fpart, fsum, fother, avg, globv, momv,
    lsem, main_s, main_r, w_s, w_r, msg_s, msg_r, st_s, st_r, g_s, g_r,
    f_s, f_r, h_s, h_r, b_s, b_r, ready, crossed,
):
    rep, me = lax.axis_index("rep"), lax.axis_index("fsdp")
    z, xh, core = rep // 4, lax.rem(rep // 2, 2), lax.rem(rep, 2)

    def flip(a, b, bits):
        out = a
        for i in range(bits):
            if b >> i & 1:
                bit = lax.rem(a // (1 << i), 2)
                out = out + (1 << i) * (1 - 2 * bit)
        return out

    peer = [flip(me, s, 3) for s in range(SHARE)]
    mate = [(flip(z, s >> 1, 3), flip(core, s & 1, 1)) for s in range(16)]

    def mate_rep(s):
        return mate[s][0] * 4 + xh * 2 + mate[s][1]

    across = z * 4 + (1 - xh) * 2 + core

    local = [
        pltpu.make_async_copy(depth, depthv, lsem.at[0]),
        pltpu.make_async_copy(trow, idxv.at[0], lsem.at[1]),
        pltpu.make_async_copy(tcol, idxv.at[1], lsem.at[2]),
        pltpu.make_async_copy(tfr, idxv.at[2], lsem.at[3]),
        pltpu.make_async_copy(tcam, idxv.at[3], lsem.at[4]),
        pltpu.make_async_copy(poses, posev, lsem.at[5]),
        pltpu.make_async_copy(gain.at[:, pl.ds(me * DS, DS)], gainv, lsem.at[6]),
        pltpu.make_async_copy(frag.at[0], fragv, lsem.at[7]),
        pltpu.make_async_copy(glob, globv, lsem.at[8]),
        pltpu.make_async_copy(mom, momv, lsem.at[9]),
        pltpu.make_async_copy(
            weight.at[0, :, pl.ds(me * DS, DS)], wv.at[pl.ds(me * ROWS, ROWS)], lsem.at[10]
        ),
    ]
    for copy in local:
        copy.start()

    barrier = pltpu.get_barrier_semaphore()
    for s in range(1, SHARE):

        @pl.when(peer[s] != 0)
        def _():
            pl.semaphore_signal(barrier, inc=1, device_id=(rep, peer[s]), device_id_type=MESH)

    @pl.when(me != 0)
    def _():
        pl.semaphore_wait(barrier, SHARE - 1)
        pl.semaphore_signal(ready, inc=1, device_id=(rep, 0), device_id_type=MESH)

    @pl.when(me == 0)
    def _():
        pl.semaphore_wait(ready, SHARE - 1)
        for s in range(1, 16):
            pl.semaphore_signal(barrier, inc=1, device_id=(mate_rep(s), me), device_id_type=MESH)
        pl.semaphore_signal(barrier, inc=1, device_id=(across, me), device_id_type=MESH)

    def remote(src, dst, send, recv, device):
        return pltpu.make_async_remote_copy(
            src_ref=src, dst_ref=dst, send_sem=send, recv_sem=recv, device_id=device, device_id_type=MESH
        )

    w_copies = [
        remote(
            weight.at[0, :, pl.ds(peer[s] * DS, DS)],
            wv.at[pl.ds(me * ROWS, ROWS)],
            w_s.at[s], w_r.at[s], (rep, peer[s]),
        )
        for s in range(1, SHARE)
    ]
    for copy in w_copies:
        copy.start()

    for i in range(5):
        local[i].wait()
    msg[me, pl.ds(0, TOK), :] = depthv[...].T.astype(BF16)
    spot = jnp.concatenate(
        [
            (idxv[3] * NFRAME + idxv[2]).astype(F32),
            idxv[1].astype(F32),
            idxv[0].astype(F32),
            jnp.zeros((10, 128), F32),
        ],
        axis=0,
    )
    msg[me, pl.ds(TOK, 16), :] = spot.astype(BF16)
    msg_copies = [
        remote(msg.at[me], msg.at[me], msg_s.at[s], msg_r.at[s], (rep, peer[s]))
        for s in range(1, SHARE)
    ]
    for copy in msg_copies:
        copy.start()

    def main_copies(c):
        out = []
        for k, (src, dst) in enumerate(((tok, tokv), (cot, cotv))):
            for s in range(SHARE):
                source = src.at[pl.ds(c * TC, TC), pl.ds(peer[s] * DS, DS)]
                target = dst.at[c, pl.ds(pl.multiple_of(me * TC, TC), TC)]
                if s == 0:
                    out.append(pltpu.make_async_copy(source, target, main_r.at[c, k, 0]))
                else:
                    out.append(
                        remote(source, target, main_s.at[c, k, s], main_r.at[c, k, s], (rep, peer[s]))
                    )
        return out

    mains = [main_copies(c) for c in range(CHUNKS)]
    for c in range(2):
        for copy in mains[c]:
            copy.start()

    local[7].wait()
    chosen[...] = fragv[block[0]]
    f_copies = [
        remote(
            chosen.at[pl.ds(mate[s][0] * FP, FP), pl.ds(mate[s][1] * 128, 128)],
            fpart.at[s],
            f_s.at[s], f_r.at[s], (mate_rep(s), me),
        )
        for s in range(1, 16)
    ]
    h_copy = remote(fsum, fother, h_s.at[0], h_r.at[0], (across, me))
    piece = (pl.ds(pl.multiple_of(z * FP, 16), FP), pl.ds(pl.multiple_of(core * 128, 128), 128))
    own = avg.at[piece]
    b_copies = [remote(own, own, b_s.at[s], b_r.at[s], (mate_rep(s), me)) for s in range(1, 16)]

    def scatter():
        @pl.when(me == 0)
        def _():
            pl.semaphore_wait(barrier, 16)
            for s in range(1, SHARE):
                pl.semaphore_signal(crossed, inc=1, device_id=(rep, peer[s]), device_id_type=MESH)

        @pl.when(me != 0)
        def _():
            pl.semaphore_wait(crossed, 1)

        for copy in f_copies:
            copy.start()

    def exchange():
        for copy in f_copies:
            copy.wait_recv()
        total = chosen[piece].astype(F32)
        for s in range(1, 16):
            total = total + fpart[s].astype(F32)
        fsum[...] = total
        h_copy.start()

    def spread_average():
        h_copy.wait_recv()
        avg[piece] = ((fsum[...] + fother[...]) * (1.0 / N_REP)).astype(BF16)
        for copy in b_copies:
            copy.start()

    def nesterov():
        for copy in b_copies:
            copy.wait_recv()
        local[8].wait()
        local[9].wait()

        def body(i, _):
            at = pl.ds(pl.multiple_of(i * 64, 64), 64)
            delta = globv[at, :] - avg[at, :].astype(F32)
            moment = MOMENTUM_RATE * momv[at, :] + delta
            new = globv[at, :] - OUTER_RATE * (MOMENTUM_RATE * moment + delta)
            mom_out[at, :] = moment
            glob_out[at, :] = new
            merged_out[0, at, :] = (
                MIX_RATE * chosen[at, :].astype(F32) + (1.0 - MIX_RATE) * new
            ).astype(BF16)
            return 0

        lax.fori_loop(0, FR // 64, body, 0)

    local[5].wait()
    pixel = lax.broadcasted_iota(jnp.int32, (1, PIX), 1)
    sub_rows = PIX // 16
    horiz = (lax.rem(pixel, 16).astype(F32) + 0.5) / (GW * 16) * 2.0 - 1.0
    vert = ((pixel // 16).astype(F32) + 0.5) / (GH * sub_rows) * 2.0 - 1.0
    table_hi[...] = jnp.zeros_like(table_hi)
    table_lo[...] = jnp.zeros_like(table_lo)

    def put(part, channel, value):
        high = value.astype(BF16)
        where = (pl.ds(part * 128, POSES), pl.ds(channel * PIX, PIX))
        table_hi[where] = high
        table_lo[where] = (value - high.astype(F32)).astype(BF16)

    def entry(k):
        return jnp.broadcast_to(posev[k], (128, POSES)).T

    for ch in range(3):
        first, second, third = entry(3 * ch), entry(3 * ch + 1), entry(3 * ch + 2)
        put(0, ch, first * horiz + second * vert + third)
        put(1, ch, first * (2.0 / GW))
        put(2, ch, second * (2.0 / GH))
        put(0, 3 + ch, entry(9 + ch))

    for copy in msg_copies:
        copy.wait_recv()

    lane = lax.broadcasted_iota(jnp.int32, (128, 128), 1).astype(F32)

    def ray_block(s, _):
        spots = msg[s, pl.ds(TOK, 16), :].astype(F32)
        for half in range(2):
            hot = jnp.where(spread(spots[half : half + 1]) == lane, 1.0, 0.0)
            left = jnp.concatenate(
                [
                    hot,
                    hot * spread(spots[2 + half : 3 + half]),
                    hot * spread(spots[4 + half : 5 + half]),
                ],
                axis=1,
            ).astype(BF16)
            geo = jnp.dot(left, table_hi[...], preferred_element_type=F32) + jnp.dot(
                left, table_lo[...], preferred_element_type=F32
            )
            d = [geo[:, i * PIX : (i + 1) * PIX] for i in range(6)]
            far = msg[s, pl.ds(half * 128, 128), :].astype(F32)
            inv = lax.rsqrt(d[0] * d[0] + d[1] * d[1] + d[2] * d[2])
            near = inv / far
            long = inv * far
            for i in range(6):
                value = (d[i] * near if i < 3 else d[i] + d[i - 3] * long).astype(BF16)
                for q in range(128 // TC):
                    c = half * (128 // TC) + q
                    start = pl.multiple_of(s * TC, TC)
                    rays_t[c, pl.ds(start, TC), pl.ds(i * PIX, PIX)] = value[q * TC : (q + 1) * TC]
        return 0

    lax.fori_loop(0, SHARE, ray_block, 0)

    def turn(k, _):
        c, b = k // (CT // 128), lax.rem(k, CT // 128)
        start = pl.multiple_of(b * 128, 128)
        rays[c, :, pl.ds(start, 128)] = rays_t[c, pl.ds(start, 128), :].T
        return 0

    lax.fori_loop(0, CHUNKS * (CT // 128), turn, 0)

    for copy in w_copies:
        copy.wait_recv()
    local[6].wait()
    local[10].wait()
    gain_row = gainv[...]
    gacc[...] = jnp.zeros_like(gacc)

    def forward(c):
        def body(b, _):
            at = pl.ds(pl.multiple_of(b * 128, 128), 128)
            lifted = jnp.dot(rays_t[c, at, :], wv[...], preferred_element_type=F32)
            hidden = tokv[c, at, :].astype(F32) + lifted
            hid[c, at, :] = hidden
            square = hidden * hidden
            cross = hidden * (cotv[c, at, :].astype(F32) * gain_row)
            q1, q2 = square[:, :128], cross[:, :128]
            for k in range(1, DS // 128):
                q1 = q1 + square[:, k * 128 : (k + 1) * 128]
                q2 = q2 + cross[:, k * 128 : (k + 1) * 128]
            stat[c, 0, pl.ds(b, 1), :] = jnp.sum(q1.T, axis=0, keepdims=True)
            stat[c, 0, pl.ds(b + CT // 128, 1), :] = jnp.sum(q2.T, axis=0, keepdims=True)
            return 0

        lax.fori_loop(0, CT // 128, body, 0)

    def stat_copies(c):
        return [
            remote(stat.at[c, 0], stat.at[c, s], st_s.at[c, s], st_r.at[c, s], (rep, peer[s]))
            for s in range(1, SHARE)
        ]

    def backward(c):
        both = stat[c, 0]
        for s in range(1, SHARE):
            both = both + stat[c, s]
        scale = lax.rsqrt(both[: CT // 128] / D + EPS)
        pull = scale * scale * scale * (both[CT // 128 :] / D)
        for b in range(CT // 128):
            wide = spread(scale[b : b + 1])
            wide_pull = spread(pull[b : b + 1])
            at = pl.ds(b * 128, 128)
            for k in range(DS // 128):
                cols = pl.ds(k * 128, 128)
                hidden = hid[c, at, cols]
                up = cotv[c, at, cols].astype(F32) * wide
                slope[at, cols] = (up * gainv[:, cols] - wide_pull * hidden).astype(BF16)
                prod = up * hidden
                part = prod[0:8]
                for i in range(1, 16):
                    part = part + prod[i * 8 : (i + 1) * 8]
                gacc[:, cols] += part

    def spend(c):
        def body(i, _):
            at = pl.ds(pl.multiple_of(i * 192, 192), 192)
            new = jnp.dot(rays[c, at, :], slope[...], preferred_element_type=F32)
            if c == 0:
                acc[at, :] = new
            else:
                acc[at, :] += new
            return 0

        lax.fori_loop(0, PIN // 192, body, 0)

    stats = [stat_copies(c) for c in range(CHUNKS)]
    for c in range(CHUNKS):
        for copy in mains[c]:
            copy.wait_recv() if copy.is_remote else copy.wait()
        if c + 2 < CHUNKS:
            for copy in mains[c]:
                if copy.is_remote:
                    copy.wait_send()
            for copy in mains[c + 2]:
                copy.start()
        forward(c)
        for copy in stats[c]:
            copy.start()
        if c == 0:
            scatter()
        if c == 1:
            exchange()
        if c == 2:
            spread_average()
        if c > 0:
            for copy in stats[c - 1]:
                copy.wait_recv()
            backward(c - 1)
            spend(c - 1)
    last = CHUNKS - 1
    for copy in stats[last]:
        copy.wait_recv()
    backward(last)

    g_copies = []
    for k in (1, 2, 3, 0):
        pair = flip(me // 2, k, 2)
        at = pl.ds(pl.multiple_of(pair * 192, 192), 192)
        grad[at, :] = (
            acc[at, :] + jnp.dot(rays[last, at, :], slope[...], preferred_element_type=F32)
        ).astype(BF16)
        for s in (2 * k, 2 * k + 1):
            source = grad.at[pl.ds(peer[s] * ROWS, ROWS)]
            target = grad_out.at[0, :, pl.ds(me * DS, DS)]
            if s == 0:
                mine = pltpu.make_async_copy(source, target, lsem.at[10])
                mine.start()
            else:
                copy = remote(source, target, g_s.at[s], g_r.at[s], (rep, peer[s]))
                copy.start()
                g_copies.append(copy)
    gain_out[...] = jnp.sum(gacc[...], axis=0, keepdims=True)
    nesterov()
    mine.wait()
    for copy in w_copies + msg_copies + f_copies + [h_copy] + b_copies:
        copy.wait_send()
    for c in range(CHUNKS):
        if c + 2 >= CHUNKS:
            for copy in mains[c]:
                if copy.is_remote:
                    copy.wait_send()
        for copy in stats[c]:
            copy.wait_send()
    for copy in g_copies:
        copy.wait()


def finish(*refs):
    ins, outs, sem = refs[:5], refs[5:10], refs[10]
    copies = [pltpu.make_async_copy(a, b, sem.at[i]) for i, (a, b) in enumerate(zip(ins, outs))]
    for copy in copies:
        copy.start()
    for copy in copies:
        copy.wait()


def shards(
    tokens, cotangent, token_row, token_col, token_frame, token_camera, pixel_depth,
    cam_poses, cam_weight, gain, frag_stack, frag_block, global_frag, momentum,
):
    dma = pltpu.SemaphoreType.DMA
    hbm = pl.BlockSpec(memory_space=pltpu.HBM)
    places = [a.reshape(2, 128) for a in (token_row, token_col, token_frame, token_camera)]
    shapes = (((1, ROWS, D), BF16), ((1, DS), F32), ((FR, 256), F32), ((FR, 256), F32), ((1, FR, 256), BF16))
    results = pl.pallas_call(
        kernel,
        name="step",
        out_shape=tuple(pltpu.VMEM(*one) for one in shapes),
        in_specs=[hbm] * 11 + [pl.BlockSpec(memory_space=pltpu.SMEM)] + [hbm] * 2,
        out_specs=(pl.BlockSpec(memory_space=pltpu.VMEM),) * 5,
        scratch_shapes=[
            pltpu.VMEM((CHUNKS, CT, DS), BF16),
            pltpu.VMEM((CHUNKS, CT, DS), BF16),
            pltpu.VMEM((PIN, DS), BF16),
            pltpu.VMEM((SHARE, MSG, 128), BF16),
            pltpu.VMEM((PIX, TOK), F32),
            pltpu.VMEM((4, 2, 128), jnp.int32),
            pltpu.VMEM((12, 1, POSES), F32),
            pltpu.VMEM((1, DS), F32),
            pltpu.VMEM((384, PIN), BF16),
            pltpu.VMEM((384, PIN), BF16),
            pltpu.VMEM((CHUNKS, CT, PIN), BF16),
            pltpu.VMEM((CHUNKS, PIN, CT), BF16),
            pltpu.VMEM((CHUNKS, CT, DS), F32),
            pltpu.VMEM((CT, DS), BF16),
            pltpu.VMEM((PIN, DS), F32),
            pltpu.VMEM((PIN, DS), BF16),
            pltpu.VMEM((8, DS), F32),
            pltpu.VMEM((CHUNKS, SHARE, 2 * CT // 128, 128), F32),
            pltpu.VMEM((6, FR, 256), BF16),
            pltpu.VMEM((FR, 256), BF16),
            pltpu.VMEM((16, FP, 128), BF16),
            pltpu.VMEM((FP, 128), F32),
            pltpu.VMEM((FP, 128), F32),
            pltpu.VMEM((FR, 256), BF16),
            pltpu.VMEM((FR, 256), F32),
            pltpu.VMEM((FR, 256), F32),
            dma((11,)),
            dma((CHUNKS, 2, SHARE)), dma((CHUNKS, 2, SHARE)),
            dma((SHARE,)), dma((SHARE,)),
            dma((SHARE,)), dma((SHARE,)),
            dma((CHUNKS, SHARE)), dma((CHUNKS, SHARE)),
            dma((SHARE,)), dma((SHARE,)),
            dma((16,)), dma((16,)),
            dma((1,)), dma((1,)),
            dma((16,)), dma((16,)),
            pltpu.SemaphoreType.REGULAR, pltpu.SemaphoreType.REGULAR,
        ],
        compiler_params=pltpu.CompilerParams(
            collective_id=0, has_side_effects=True, vmem_limit_bytes=44 << 20
        ),
        cost_estimate=pl.CostEstimate(flops=6 << 30, bytes_accessed=20 << 20, transcendentals=0),
    )(
        *[
            pltpu.with_memory_space_constraint(a, pltpu.HBM)
            for a in (
                tokens, cotangent, *places, pixel_depth, cam_poses.transpose(1, 0, 2), cam_weight, gain, frag_stack
            )
        ],
        *[pltpu.with_memory_space_constraint(a, pltpu.HBM) for a in (frag_block, global_frag, momentum)],
    )
    return pl.pallas_call(
        finish,
        name="finish",
        out_shape=tuple(jax.ShapeDtypeStruct(*one) for one in shapes),
        in_specs=[pl.BlockSpec(memory_space=pltpu.VMEM)] * 5,
        out_specs=(pl.BlockSpec(memory_space=pltpu.HBM),) * 5,
        scratch_shapes=[dma((5,))],
    )(*[pltpu.with_memory_space_constraint(a, pltpu.VMEM) for a in results])


def solution(mesh):
    placed = (
        P(("rep", "fsdp"), None),
        P(("rep", "fsdp"), None),
        P(("rep", "fsdp")),
        P(("rep", "fsdp")),
        P(("rep", "fsdp")),
        P(("rep", "fsdp")),
        P(None, ("rep", "fsdp")),
        P("rep", None, None),
        P("rep", "fsdp", None),
        P("rep", None),
        P("rep", None, "fsdp", None),
        P(),
        P("fsdp", None),
        P("fsdp", None),
    )
    return jax.shard_map(
        shards,
        mesh=mesh,
        in_specs=placed,
        out_specs=(
            P("rep", "fsdp", None),
            P("rep", "fsdp"),
            P("fsdp", None),
            P("fsdp", None),
            P("rep", "fsdp", None),
        ),
        check_vma=False,
    )
```

```python
import jax
import jax.numpy as jnp
from jax import lax
from jax.experimental import pallas as pl
from jax.experimental.pallas import tpu as pltpu
from jax.sharding import PartitionSpec as P

D = 5120
PIX = 128
NFRAME = 24
GH = 44
GW = 80
PIN = 768
POSES = 96
N_REP = 32
SHARE = 8
DS = D // SHARE
ROWS = PIN // SHARE
TOK = 256
FR = 640
FP = 80
MSG = TOK + 16

WIDTH = (512, 384, 384)
BASE = (0, 2048, 3584)
PAIR = ((0, 1, 2, 3), (0, 1, 4, 5), (0, 3, 4, 7))
TWIN = (4, 3, 1)
CLASSES = range(3)
GROUP = 4
GT = GROUP * TOK

SIZES = (64, 64, 64, 32, 32)
STARTS = tuple(sum(SIZES[:c]) for c in range(len(SIZES)))
CHUNKS = len(SIZES)
AHEAD = 2

EPS = 1e-06
MOMENTUM_RATE = 0.9
OUTER_RATE = 0.7
MIX_RATE = 0.5

MESH = pl.DeviceIdType.MESH
F32 = jnp.float32
BF16 = jnp.bfloat16


def spread(row):
    return jnp.broadcast_to(row, (128, 128)).T


def flip(a, b):
    out = a
    for i in range(3):
        if b >> i & 1:
            out = out + (1 << i) * (1 - 2 * lax.rem(a // (1 << i), 2))
    return out


def gain_tile(device, place):
    x, y = device // 4, device % 4
    slots = (y, x * 2 + ((y >> 1 ^ y) & 1), x * 2 + (y >> 1))
    for k in CLASSES:
        tiles = WIDTH[k] // 128
        if place < tiles:
            return BASE[k] // 128 + slots[k] * tiles + place
        place -= tiles


def kernel(
    tok, cot, trow, tcol, tfr, tcam, depth, poses, weight, gain, frag, block, glob, mom,
    grad_out, gain_out, glob_out, mom_out, merged_out,
    tok_a, tok_b, tok_c, cot_a, cot_b, cot_c, w_a, w_b, w_c, rt_a, rt_b, rt_c, rays_a, rays_b, rays_c,
    hid_a, hid_b, hid_c, slope_a, slope_b, slope_c, acc_a, acc_b, acc_c, send_a, send_b, send_c,
    part_a, part_b, part_c, last_a, last_b, last_c, gacc_a, gacc_b, gacc_c, gain_a, gain_b, gain_c,
    msg, depthv, idxv, posev, table_hi, table_lo, rays_all, stat, scales, pulls, gains, gsum,
    fragv, chosen, fpart, fsum, fother, avg, globv, momv,
    lsem, wl_s, gl_s, main_s, main_r, w_s, w_r, v_s, v_r, msg_s, msg_r, st_s, st_r, p_s, p_r, g_s, g_r,
    gg_s, gg_r, f_s, f_r, h_s, h_r, b_s, b_r, ready, crossed,
):
    tokv, cotv, wv = (tok_a, tok_b, tok_c), (cot_a, cot_b, cot_c), (w_a, w_b, w_c)
    rays_t, rays, hid = (rt_a, rt_b, rt_c), (rays_a, rays_b, rays_c), (hid_a, hid_b, hid_c)
    slope, acc, send = (slope_a, slope_b, slope_c), (acc_a, acc_b, acc_c), (send_a, send_b, send_c)
    part, last_out, gacc = (part_a, part_b, part_c), (last_a, last_b, last_c), (gacc_a, gacc_b, gacc_c)
    gainv = (gain_a, gain_b, gain_c)

    rep, me = lax.axis_index("rep"), lax.axis_index("fsdp")
    z, xh, core = rep // 4, lax.rem(rep // 2, 2), lax.rem(rep, 2)
    x, y = me // 4, lax.rem(me, 4)
    high, low = y // 2, lax.rem(y, 2)
    odd = high + low - 2 * high * low
    peer = [flip(me, s) for s in range(SHARE)]
    place = (y, x * 2 + odd, x * 2 + high)

    def member(k, i):
        if k == 0:
            return x * 4 + i
        s = i & 1
        if k == 1:
            return (i >> 1) * 4 + 2 * high + (1 - high if s else high)
        return (i >> 1) * 4 + 2 * s + (1 - odd if s else odd)

    def columns(k, at):
        return pl.ds(pl.multiple_of(BASE[k] + at * WIDTH[k], 128), WIDTH[k])

    def rows_of(device):
        return pl.ds(pl.multiple_of(device * ROWS, 32), ROWS)

    mate = [(flip(z, s >> 1), flip(core, s & 1)) for s in range(16)]

    def mate_rep(s):
        return mate[s][0] * 4 + xh * 2 + mate[s][1]

    across = z * 4 + (1 - xh) * 2 + core

    local = [
        pltpu.make_async_copy(depth, depthv, lsem.at[0]),
        pltpu.make_async_copy(trow, idxv.at[0], lsem.at[1]),
        pltpu.make_async_copy(tcol, idxv.at[1], lsem.at[2]),
        pltpu.make_async_copy(tfr, idxv.at[2], lsem.at[3]),
        pltpu.make_async_copy(tcam, idxv.at[3], lsem.at[4]),
        pltpu.make_async_copy(poses, posev, lsem.at[5]),
        pltpu.make_async_copy(frag.at[0], fragv, lsem.at[6]),
        pltpu.make_async_copy(glob, globv, lsem.at[7]),
        pltpu.make_async_copy(mom, momv, lsem.at[8]),
    ]
    for copy in local:
        copy.start()
    w_local = [
        pltpu.make_async_copy(weight.at[0, :, columns(k, place[k])], wv[k].at[rows_of(me)], wl_s.at[k])
        for k in CLASSES
    ]
    gain_local = [
        pltpu.make_async_copy(gain.at[:, columns(k, place[k])], gainv[k], gl_s.at[k]) for k in CLASSES
    ]
    for copy in w_local + gain_local:
        copy.start()

    barrier = pltpu.get_barrier_semaphore()
    for s in range(1, SHARE):

        @pl.when(peer[s] != 0)
        def _():
            pl.semaphore_signal(barrier, inc=1, device_id=(rep, peer[s]), device_id_type=MESH)

    @pl.when(me != 0)
    def _():
        pl.semaphore_wait(barrier, SHARE - 1)
        pl.semaphore_signal(ready, inc=1, device_id=(rep, 0), device_id_type=MESH)

    @pl.when(me == 0)
    def _():
        pl.semaphore_wait(ready, SHARE - 1)
        for s in range(1, 16):
            pl.semaphore_signal(barrier, inc=1, device_id=(mate_rep(s), me), device_id_type=MESH)
        pl.semaphore_signal(barrier, inc=1, device_id=(across, me), device_id_type=MESH)

    def remote(src, dst, send, recv, device):
        return pltpu.make_async_remote_copy(
            src_ref=src, dst_ref=dst, send_sem=send, recv_sem=recv, device_id=device, device_id_type=MESH
        )

    w_copies = [
        [
            remote(
                weight.at[0, :, columns(k, flip(place[k], e))],
                wv[k].at[rows_of(me)],
                w_s.at[k, e], w_r.at[k, e], (rep, peer[PAIR[k][e]]),
            )
            for e in range(1, GROUP)
        ]
        for k in CLASSES
    ]
    for e in range(GROUP - 1):
        for k in CLASSES:
            w_copies[k][e].start()
    v_copies = [
        [
            remote(
                weight.at[0, :, columns(k, place[k])] if e == 0 else wv[k].at[rows_of(peer[PAIR[k][e]])],
                wv[k].at[rows_of(peer[PAIR[k][e]])],
                v_s.at[k, e], v_r.at[k, e], (rep, peer[TWIN[k]]),
            )
            for e in range(GROUP)
        ]
        for k in CLASSES
    ]
    for k in CLASSES:
        v_copies[k][0].start()

    for i in range(5):
        local[i].wait()
    msg[me, pl.ds(0, TOK), :] = depthv[...].T.astype(BF16)
    spot = jnp.concatenate(
        [
            (idxv[3] * NFRAME + idxv[2]).astype(F32),
            idxv[1].astype(F32),
            idxv[0].astype(F32),
            jnp.zeros((10, 128), F32),
        ],
        axis=0,
    )
    msg[me, pl.ds(TOK, 16), :] = spot.astype(BF16)
    near = [s for s in range(1, SHARE) if s != 6]
    msg_copies = [
        remote(msg.at[me], msg.at[me], msg_s.at[s], msg_r.at[s], (rep, peer[s])) for s in near
    ]
    for copy in msg_copies:
        copy.start()

    def main_copies(c):
        near_ones, far_ones = [], []
        for n, (src, dsts) in enumerate(((tok, tokv), (cot, cotv))):
            for e in (1, 2, 3, 0):
                for k in CLASSES:
                    source = src.at[pl.ds(STARTS[c], SIZES[c]), columns(k, flip(place[k], e))]
                    start = pl.multiple_of(GROUP * STARTS[c] + place[k] * SIZES[c], 32)
                    target = dsts[k].at[pl.ds(start, SIZES[c])]
                    if e == 0:
                        near_ones.append(pltpu.make_async_copy(source, target, main_r.at[c, n, k, 0]))
                    else:
                        far_ones.append(
                            remote(
                                source, target, main_s.at[c, n, k, e], main_r.at[c, n, k, e],
                                (rep, peer[PAIR[k][e]]),
                            )
                        )
        return near_ones, far_ones

    mains = [main_copies(c) for c in range(CHUNKS)]

    def start_main(c):
        for copy in mains[c][1] + mains[c][0]:
            copy.start()

    start_main(0)

    local[6].wait()
    chosen[...] = fragv[block[0]]
    f_copies = [
        remote(
            chosen.at[pl.ds(mate[s][0] * FP, FP), pl.ds(mate[s][1] * 128, 128)],
            fpart.at[s],
            f_s.at[s], f_r.at[s], (mate_rep(s), me),
        )
        for s in range(1, 16)
    ]
    h_copy = remote(fsum, fother, h_s.at[0], h_r.at[0], (across, me))
    piece = (pl.ds(pl.multiple_of(z * FP, 16), FP), pl.ds(pl.multiple_of(core * 128, 128), 128))
    own = avg.at[piece]
    b_copies = [remote(own, own, b_s.at[s], b_r.at[s], (mate_rep(s), me)) for s in range(1, 16)]

    def scatter():
        @pl.when(me == 0)
        def _():
            pl.semaphore_wait(barrier, 16)
            for s in range(1, SHARE):
                pl.semaphore_signal(crossed, inc=1, device_id=(rep, peer[s]), device_id_type=MESH)

        @pl.when(me != 0)
        def _():
            pl.semaphore_wait(crossed, 1)

        for copy in f_copies:
            copy.start()

    def exchange():
        for copy in f_copies:
            copy.wait_recv()
        total = chosen[piece].astype(F32)
        for s in range(1, 16):
            total = total + fpart[s].astype(F32)
        fsum[...] = total
        h_copy.start()

    def spread_average():
        h_copy.wait_recv()
        avg[piece] = ((fsum[...] + fother[...]) * (1.0 / N_REP)).astype(BF16)
        for copy in b_copies:
            copy.start()

    def nesterov():
        for copy in b_copies:
            copy.wait_recv()
        local[7].wait()
        local[8].wait()

        def body(i, _):
            at = pl.ds(pl.multiple_of(i * 64, 64), 64)
            delta = globv[at, :] - avg[at, :].astype(F32)
            moment = MOMENTUM_RATE * momv[at, :] + delta
            new = globv[at, :] - OUTER_RATE * (MOMENTUM_RATE * moment + delta)
            mom_out[at, :] = moment
            glob_out[at, :] = new
            merged_out[0, at, :] = (
                MIX_RATE * chosen[at, :].astype(F32) + (1.0 - MIX_RATE) * new
            ).astype(BF16)
            return 0

        lax.fori_loop(0, FR // 64, body, 0)

    local[5].wait()
    pixel = lax.broadcasted_iota(jnp.int32, (1, PIX), 1)
    sub_rows = PIX // 16
    horiz = (lax.rem(pixel, 16).astype(F32) + 0.5) / (GW * 16) * 2.0 - 1.0
    vert = ((pixel // 16).astype(F32) + 0.5) / (GH * sub_rows) * 2.0 - 1.0
    table_hi[...] = jnp.zeros_like(table_hi)
    table_lo[...] = jnp.zeros_like(table_lo)

    def put(part, channel, value):
        high = value.astype(BF16)
        where = (pl.ds(part * 128, POSES), pl.ds(channel * PIX, PIX))
        table_hi[where] = high
        table_lo[where] = (value - high.astype(F32)).astype(BF16)

    def entry(k):
        return jnp.broadcast_to(posev[k], (128, POSES)).T

    for ch in range(3):
        first, second, third = entry(3 * ch), entry(3 * ch + 1), entry(3 * ch + 2)
        put(0, ch, first * horiz + second * vert + third)
        put(1, ch, first * (2.0 / GW))
        put(2, ch, second * (2.0 / GH))
        put(0, 3 + ch, entry(9 + ch))

    for e in range(1, GROUP):
        for k in CLASSES:
            w_copies[k][e - 1].wait_recv()
            v_copies[k][e].start()
    for c in range(1, AHEAD):
        start_main(c)

    for copy in msg_copies:
        copy.wait_recv()

    lane = lax.broadcasted_iota(jnp.int32, (128, 128), 1).astype(F32)

    def ray_block(s, _):
        spots = msg[s, pl.ds(TOK, 16), :].astype(F32)
        for half in range(2):
            hot = jnp.where(spread(spots[half : half + 1]) == lane, 1.0, 0.0)
            left = jnp.concatenate(
                [
                    hot,
                    hot * spread(spots[2 + half : 3 + half]),
                    hot * spread(spots[4 + half : 5 + half]),
                ],
                axis=1,
            ).astype(BF16)
            geo = jnp.dot(left, table_hi[...], preferred_element_type=F32) + jnp.dot(
                left, table_lo[...], preferred_element_type=F32
            )
            d = [geo[:, i * PIX : (i + 1) * PIX] for i in range(6)]
            far = msg[s, pl.ds(half * 128, 128), :].astype(F32)
            inv = lax.rsqrt(d[0] * d[0] + d[1] * d[1] + d[2] * d[2])
            close = inv / far
            long = inv * far
            for i in range(6):
                value = d[i] * close if i < 3 else d[i] + d[i - 3] * long
                rays_all[s, pl.ds(half * 128, 128), pl.ds(i * PIX, PIX)] = value.astype(BF16)
        return 0

    def ray_step(n, _):
        return ray_block(lax.rem(me + n, SHARE), 0)

    msg[peer[6]] = msg[me]
    lax.fori_loop(0, SHARE, ray_step, 0)

    for k in CLASSES:
        for i in range(GROUP):
            for c in range(CHUNKS):
                at = GROUP * STARTS[c] + i * SIZES[c]
                rays_t[k][pl.ds(at, SIZES[c]), :] = rays_all[member(k, i), pl.ds(STARTS[c], SIZES[c]), :]

        def turn(b, _, k=k):
            at = pl.ds(pl.multiple_of(b * 128, 128), 128)
            rays[k][:, at] = rays_t[k][at, :].T
            return 0

        lax.fori_loop(0, GT // 128, turn, 0)

    for k in CLASSES:
        w_local[k].wait()
        gain_local[k].wait()
        gacc[k][...] = jnp.zeros_like(gacc[k])
        for copy in v_copies[k]:
            copy.wait_recv()

    wide_lane = lax.broadcasted_iota(jnp.int32, (1, 128), 1)

    def forward(c):
        size = SIZES[c]
        count = 128 // size
        stat[c, 0] = jnp.zeros((SHARE, 128), F32)
        for k in CLASSES:
            for b in range(GROUP * size // 128):
                at = pl.ds(GROUP * STARTS[c] + b * 128, 128)
                lifted = jnp.dot(rays_t[k][at, :], wv[k][...], preferred_element_type=F32)
                hidden = tokv[k][at, :].astype(F32) + lifted
                hid[k][at, :] = hidden
                square = hidden * hidden
                cross = hidden * (cotv[k][at, :].astype(F32) * gainv[k][...])
                q1, q2 = square[:, :128], cross[:, :128]
                for t in range(1, WIDTH[k] // 128):
                    q1 = q1 + square[:, t * 128 : (t + 1) * 128]
                    q2 = q2 + cross[:, t * 128 : (t + 1) * 128]
                r1 = jnp.sum(q1.T, axis=0, keepdims=True)
                r2 = jnp.sum(q2.T, axis=0, keepdims=True)
                for j in range(count):
                    one = pltpu.roll(r1, (128 - j * size) % 128, 1)
                    two = pltpu.roll(r2, (192 - j * size) % 128, 1)
                    source = pl.ds(member(k, b * count + j), 1)
                    stat[c, 0, source, :] += jnp.where(wide_lane < 64, one, two)

    def stat_copies(c):
        return [
            remote(stat.at[c, 0], stat.at[c, s], st_s.at[c, s], st_r.at[c, s], (rep, peer[s]))
            for s in range(1, SHARE)
        ]

    def backward(c):
        size = SIZES[c]
        count = 128 // size
        both = stat[c, 0]
        for s in range(1, SHARE):
            both = both + stat[c, s]
        scale = lax.rsqrt(both / D + EPS)
        scales[...] = scale
        pulls[...] = scale * scale * scale * (pltpu.roll(both, 64, 1) / D)

        def gather(ref, k, b):
            row = ref[pl.ds(member(k, b * count), 1), :]
            for j in range(1, count):
                other = pltpu.roll(ref[pl.ds(member(k, b * count + j), 1), :], j * size, 1)
                row = jnp.where(wide_lane < j * size, row, other)
            return spread(row)

        for k in CLASSES:
            for b in range(GROUP * size // 128):
                wide = gather(scales, k, b)
                wide_pull = gather(pulls, k, b)
                at = pl.ds(GROUP * STARTS[c] + b * 128, 128)
                for t in range(WIDTH[k] // 128):
                    cols = pl.ds(t * 128, 128)
                    hidden = hid[k][at, cols]
                    up = cotv[k][at, cols].astype(F32) * wide
                    slope[k][pl.ds(b * 128, 128), cols] = (
                        up * gainv[k][:, cols] - wide_pull * hidden
                    ).astype(BF16)
                    prod = up * hidden
                    part_sum = prod[0:8]
                    for i in range(1, 16):
                        part_sum = part_sum + prod[i * 8 : (i + 1) * 8]
                    gacc[k][:, cols] += part_sum

    def product(c, k, at):
        count = GROUP * SIZES[c]
        return jnp.dot(
            rays[k][at, pl.ds(GROUP * STARTS[c], count)],
            slope[k][pl.ds(0, count), :],
            preferred_element_type=F32,
        )

    def spend(c):
        for k in CLASSES:

            def body(i, _, k=k):
                at = pl.ds(pl.multiple_of(i * 192, 192), 192)
                if c == 0:
                    acc[k][at, :] = product(c, k, at)
                else:
                    acc[k][at, :] += product(c, k, at)
                return 0

            lax.fori_loop(0, PIN // 192, body, 0)

    stats = [stat_copies(c) for c in range(CHUNKS)]
    for c in range(CHUNKS):
        for copy in mains[c][1]:
            copy.wait_recv()
        for copy in mains[c][0]:
            copy.wait()
        if c + AHEAD < CHUNKS:
            for copy in mains[c][1]:
                copy.wait_send()
            start_main(c + AHEAD)
        forward(c)
        for copy in stats[c]:
            copy.start()
        if c == 0:
            scatter()
        if c == 1:
            exchange()
        if c == 2:
            spread_average()
        if c > 0:
            for copy in stats[c - 1]:
                copy.wait_recv()
            backward(c - 1)
            spend(c - 1)
    last = CHUNKS - 1
    for copy in stats[last]:
        copy.wait_recv()
    backward(last)

    p_copies = []
    for k in CLASSES:
        for e in range(GROUP):
            at = rows_of(peer[TWIN[k] ^ PAIR[k][e]])
            send[k][e] = (acc[k][at, :] + product(last, k, at)).astype(BF16)
            copy = remote(send[k].at[e], part[k].at[e], p_s.at[k, e], p_r.at[k, e], (rep, peer[TWIN[k]]))
            copy.start()
            p_copies.append(copy)
    for k in CLASSES:
        for t in range(WIDTH[k] // 128):
            n = sum(WIDTH[:k]) // 128 + t
            gains[me, pl.ds(n, 1), :] = jnp.sum(gacc[k][:, pl.ds(t * 128, 128)], axis=0, keepdims=True)
    gain_copies = [
        remote(gains.at[me], gains.at[me], gg_s.at[s], gg_r.at[s], (rep, peer[s])) for s in range(1, SHARE)
    ]
    for copy in gain_copies:
        copy.start()
    g_copies = []
    for e in (1, 2, 3, 0):
        for k in CLASSES:
            at = rows_of(peer[PAIR[k][e]])
            value = acc[k][at, :] + product(last, k, at)
            p_copies[k * GROUP + e].wait_recv()
            value = (value + part[k][e].astype(F32)).astype(BF16)
            if e == 0:
                grad_out[0, :, columns(k, place[k])] = value
            else:
                last_out[k][e - 1] = value
                copy = remote(
                    last_out[k].at[e - 1], grad_out.at[0, :, columns(k, place[k])],
                    g_s.at[k, e], g_r.at[k, e], (rep, peer[PAIR[k][e]]),
                )
                copy.start()
                g_copies.append(copy)
    nesterov()
    for copy in gain_copies:
        copy.wait_recv()
    seen = set()
    for s in range(SHARE):
        for n in range(10):
            tile = pl.ds(gain_tile(s, n), 1)
            value = gains[s, pl.ds(n, 1), :]
            gsum[tile, :] = gsum[tile, :] + value if gain_tile(s, n) in seen else value
            seen.add(gain_tile(s, n))
    for t in range(DS // 128):
        gain_out[:, pl.ds(t * 128, 128)] = gsum[pl.ds(me * (DS // 128) + t, 1), :]

    for k in CLASSES:
        for copy in w_copies[k] + v_copies[k]:
            copy.wait_send()
    for copy in msg_copies + p_copies + gain_copies + f_copies + [h_copy] + b_copies:
        copy.wait_send()
    for c in range(CHUNKS):
        if c + AHEAD >= CHUNKS:
            for copy in mains[c][1]:
                copy.wait_send()
        for copy in stats[c]:
            copy.wait_send()
    for copy in g_copies:
        copy.wait()


def finish(*refs):
    ins, outs, sem = refs[:5], refs[5:10], refs[10]
    copies = [pltpu.make_async_copy(a, b, sem.at[i]) for i, (a, b) in enumerate(zip(ins, outs))]
    for copy in copies:
        copy.start()
    for copy in copies:
        copy.wait()


def shards(
    tokens, cotangent, token_row, token_col, token_frame, token_camera, pixel_depth,
    cam_poses, cam_weight, gain, frag_stack, frag_block, global_frag, momentum,
):
    dma = pltpu.SemaphoreType.DMA
    hbm = pl.BlockSpec(memory_space=pltpu.HBM)
    places = [a.reshape(2, 128) for a in (token_row, token_col, token_frame, token_camera)]
    shapes = (((1, ROWS, D), BF16), ((1, DS), F32), ((FR, 256), F32), ((FR, 256), F32), ((1, FR, 256), BF16))
    results = pl.pallas_call(
        kernel,
        name="step",
        out_shape=tuple(pltpu.VMEM(*one) for one in shapes),
        in_specs=[hbm] * 11 + [pl.BlockSpec(memory_space=pltpu.SMEM)] + [hbm] * 2,
        out_specs=(pl.BlockSpec(memory_space=pltpu.VMEM),) * 5,
        scratch_shapes=[
            *[pltpu.VMEM((GT, w), BF16) for w in WIDTH],
            *[pltpu.VMEM((GT, w), BF16) for w in WIDTH],
            *[pltpu.VMEM((PIN, w), BF16) for w in WIDTH],
            *[pltpu.VMEM((GT, PIN), BF16) for w in WIDTH],
            *[pltpu.VMEM((PIN, GT), BF16) for w in WIDTH],
            *[pltpu.VMEM((GT, w), F32) for w in WIDTH],
            *[pltpu.VMEM((GROUP * max(SIZES), w), BF16) for w in WIDTH],
            *[pltpu.VMEM((PIN, w), F32) for w in WIDTH],
            *[pltpu.VMEM((GROUP, ROWS, w), BF16) for w in WIDTH],
            *[pltpu.VMEM((GROUP, ROWS, w), BF16) for w in WIDTH],
            *[pltpu.VMEM((GROUP - 1, ROWS, w), BF16) for w in WIDTH],
            *[pltpu.VMEM((8, w), F32) for w in WIDTH],
            *[pltpu.VMEM((1, w), F32) for w in WIDTH],
            pltpu.VMEM((SHARE, MSG, 128), BF16),
            pltpu.VMEM((PIX, TOK), F32),
            pltpu.VMEM((4, 2, 128), jnp.int32),
            pltpu.VMEM((12, 1, POSES), F32),
            pltpu.VMEM((384, PIN), BF16),
            pltpu.VMEM((384, PIN), BF16),
            pltpu.VMEM((SHARE, TOK, PIN), BF16),
            pltpu.VMEM((CHUNKS, SHARE, SHARE, 128), F32),
            pltpu.VMEM((SHARE, 128), F32),
            pltpu.VMEM((SHARE, 128), F32),
            pltpu.VMEM((SHARE, 16, 128), F32),
            pltpu.VMEM((D // 128, 128), F32),
            pltpu.VMEM((6, FR, 256), BF16),
            pltpu.VMEM((FR, 256), BF16),
            pltpu.VMEM((16, FP, 128), BF16),
            pltpu.VMEM((FP, 128), F32),
            pltpu.VMEM((FP, 128), F32),
            pltpu.VMEM((FR, 256), BF16),
            pltpu.VMEM((FR, 256), F32),
            pltpu.VMEM((FR, 256), F32),
            dma((9,)), dma((3,)), dma((3,)),
            dma((CHUNKS, 2, 3, GROUP)), dma((CHUNKS, 2, 3, GROUP)),
            dma((3, GROUP)), dma((3, GROUP)),
            dma((3, GROUP)), dma((3, GROUP)),
            dma((SHARE,)), dma((SHARE,)),
            dma((CHUNKS, SHARE)), dma((CHUNKS, SHARE)),
            dma((3, GROUP)), dma((3, GROUP)),
            dma((3, GROUP)), dma((3, GROUP)),
            dma((SHARE,)), dma((SHARE,)),
            dma((16,)), dma((16,)),
            dma((1,)), dma((1,)),
            dma((16,)), dma((16,)),
            pltpu.SemaphoreType.REGULAR, pltpu.SemaphoreType.REGULAR,
        ],
        compiler_params=pltpu.CompilerParams(
            collective_id=0, has_side_effects=True, vmem_limit_bytes=56 << 20
        ),
        cost_estimate=pl.CostEstimate(flops=6 << 30, bytes_accessed=20 << 20, transcendentals=0),
    )(
        *[
            pltpu.with_memory_space_constraint(a, pltpu.HBM)
            for a in (
                tokens, cotangent, *places, pixel_depth, cam_poses.transpose(1, 0, 2), cam_weight, gain, frag_stack
            )
        ],
        *[pltpu.with_memory_space_constraint(a, pltpu.HBM) for a in (frag_block, global_frag, momentum)],
    )
    return pl.pallas_call(
        finish,
        name="finish",
        out_shape=tuple(jax.ShapeDtypeStruct(*one) for one in shapes),
        in_specs=[pl.BlockSpec(memory_space=pltpu.VMEM)] * 5,
        out_specs=(pl.BlockSpec(memory_space=pltpu.HBM),) * 5,
        scratch_shapes=[dma((5,))],
    )(*[pltpu.with_memory_space_constraint(a, pltpu.VMEM) for a in results])


def solution(mesh):
    placed = (
        P(("rep", "fsdp"), None),
        P(("rep", "fsdp"), None),
        P(("rep", "fsdp")),
        P(("rep", "fsdp")),
        P(("rep", "fsdp")),
        P(("rep", "fsdp")),
        P(None, ("rep", "fsdp")),
        P("rep", None, None),
        P("rep", "fsdp", None),
        P("rep", None),
        P("rep", None, "fsdp", None),
        P(),
        P("fsdp", None),
        P("fsdp", None),
    )
    return jax.shard_map(
        shards,
        mesh=mesh,
        in_specs=placed,
        out_specs=(
            P("rep", "fsdp", None),
            P("rep", "fsdp"),
            P("fsdp", None),
            P("fsdp", None),
            P("rep", "fsdp", None),
        ),
        check_vma=False,
    )
```

```python
import jax
import jax.numpy as jnp
from jax import lax
from jax.experimental import pallas as pl
from jax.experimental.pallas import tpu as pltpu
from jax.sharding import PartitionSpec as P

D = 5120
PIX = 128
NFRAME = 24
GH = 44
GW = 80
PIN = 768
POSES = 96
N_REP = 32
SHARE = 8
DS = D // SHARE
ROWS = PIN // SHARE
TOK = 256
FR = 640
FP = 80
MSG = TOK + 16

WIDTH = (512, 384, 384)
BASE = (0, 2048, 3584)
PAIR = ((0, 1, 2, 3), (0, 1, 4, 5), (0, 3, 4, 7))
TWIN = (4, 3, 1)
CLASSES = range(3)
GROUP = 4
GT = GROUP * TOK

SIZES = (64, 64, 64, 64)
STARTS = tuple(sum(SIZES[:c]) for c in range(len(SIZES)))
CHUNKS = len(SIZES)
ORDER = (((0,), (), (1,), (2, 3), (), ()), ((0,), (1, 2), (3,), (), (), ()))

EPS = 1e-06
MOMENTUM_RATE = 0.9
OUTER_RATE = 0.7
MIX_RATE = 0.5

MESH = pl.DeviceIdType.MESH
F32 = jnp.float32
BF16 = jnp.bfloat16


def spread(row):
    return jnp.broadcast_to(row, (128, 128)).T


def flip(a, b):
    out = a
    for i in range(3):
        if b >> i & 1:
            out = out + (1 << i) * (1 - 2 * lax.rem(a // (1 << i), 2))
    return out


def gain_tile(device, place):
    x, y = device // 4, device % 4
    slots = (y, x * 2 + ((y >> 1 ^ y) & 1), x * 2 + (y >> 1))
    for k in CLASSES:
        tiles = WIDTH[k] // 128
        if place < tiles:
            return BASE[k] // 128 + slots[k] * tiles + place
        place -= tiles


def kernel(
    tok, cot, trow, tcol, tfr, tcam, depth, poses, weight, gain, frag, block, glob, mom,
    grad_out, gain_out, glob_out, mom_out, merged_out,
    tok_a, tok_b, tok_c, cot_a, cot_b, cot_c, w_a, w_b, w_c, rt_a, rt_b, rt_c, rays_a, rays_b, rays_c,
    hid_a, hid_b, hid_c, slope_a, slope_b, slope_c, acc_a, acc_b, acc_c, send_a, send_b, send_c,
    part_a, part_b, part_c, last_a, last_b, last_c, gacc_a, gacc_b, gacc_c, gain_a, gain_b, gain_c,
    msg, depthv, idxv, posev, table_hi, table_lo, rays_all, stat, scales, pulls, gains, gsum,
    fragv, chosen, fpart, fsum, fother, avg, globv, momv,
    lsem, wl_s, gl_s, main_s, main_r, w_s, w_r, v_s, v_r, msg_s, msg_r, st_s, st_r, p_s, p_r, g_s, g_r,
    gg_s, gg_r, f_s, f_r, h_s, h_r, b_s, b_r, ready, crossed,
):
    tokv, cotv, wv = (tok_a, tok_b, tok_c), (cot_a, cot_b, cot_c), (w_a, w_b, w_c)
    rays_t, rays, hid = (rt_a, rt_b, rt_c), (rays_a, rays_b, rays_c), (hid_a, hid_b, hid_c)
    slope, acc, send = (slope_a, slope_b, slope_c), (acc_a, acc_b, acc_c), (send_a, send_b, send_c)
    part, last_out, gacc = (part_a, part_b, part_c), (last_a, last_b, last_c), (gacc_a, gacc_b, gacc_c)
    gainv = (gain_a, gain_b, gain_c)

    rep, me = lax.axis_index("rep"), lax.axis_index("fsdp")
    z, xh, core = rep // 4, lax.rem(rep // 2, 2), lax.rem(rep, 2)
    x, y = me // 4, lax.rem(me, 4)
    high, low = y // 2, lax.rem(y, 2)
    odd = high + low - 2 * high * low
    peer = [flip(me, s) for s in range(SHARE)]
    place = (y, x * 2 + odd, x * 2 + high)

    def member(k, i):
        if k == 0:
            return x * 4 + i
        s = i & 1
        if k == 1:
            return (i >> 1) * 4 + 2 * high + (1 - high if s else high)
        return (i >> 1) * 4 + 2 * s + (1 - odd if s else odd)

    def columns(k, at):
        return pl.ds(pl.multiple_of(BASE[k] + at * WIDTH[k], 128), WIDTH[k])

    def rows_of(device):
        return pl.ds(pl.multiple_of(device * ROWS, 32), ROWS)

    mate = [(flip(z, s >> 1), flip(core, s & 1)) for s in range(16)]

    def mate_rep(s):
        return mate[s][0] * 4 + xh * 2 + mate[s][1]

    across = z * 4 + (1 - xh) * 2 + core

    local = [
        pltpu.make_async_copy(depth, depthv, lsem.at[0]),
        pltpu.make_async_copy(trow, idxv.at[0], lsem.at[1]),
        pltpu.make_async_copy(tcol, idxv.at[1], lsem.at[2]),
        pltpu.make_async_copy(tfr, idxv.at[2], lsem.at[3]),
        pltpu.make_async_copy(tcam, idxv.at[3], lsem.at[4]),
        pltpu.make_async_copy(poses, posev, lsem.at[5]),
        pltpu.make_async_copy(frag.at[0], fragv, lsem.at[6]),
        pltpu.make_async_copy(glob, globv, lsem.at[7]),
        pltpu.make_async_copy(mom, momv, lsem.at[8]),
    ]
    for copy in local:
        copy.start()
    w_local = [
        pltpu.make_async_copy(weight.at[0, :, columns(k, place[k])], wv[k].at[rows_of(me)], wl_s.at[k])
        for k in CLASSES
    ]
    gain_local = [
        pltpu.make_async_copy(gain.at[:, columns(k, place[k])], gainv[k], gl_s.at[k]) for k in CLASSES
    ]
    for copy in w_local + gain_local:
        copy.start()

    barrier = pltpu.get_barrier_semaphore()
    for s in range(1, SHARE):

        @pl.when(peer[s] != 0)
        def _():
            pl.semaphore_signal(barrier, inc=1, device_id=(rep, peer[s]), device_id_type=MESH)

    @pl.when(me != 0)
    def _():
        pl.semaphore_wait(barrier, SHARE - 1)
        pl.semaphore_signal(ready, inc=1, device_id=(rep, 0), device_id_type=MESH)

    @pl.when(me == 0)
    def _():
        pl.semaphore_wait(ready, SHARE - 1)
        for s in range(1, 16):
            pl.semaphore_signal(barrier, inc=1, device_id=(mate_rep(s), me), device_id_type=MESH)
        pl.semaphore_signal(barrier, inc=1, device_id=(across, me), device_id_type=MESH)

    def remote(src, dst, send, recv, device):
        return pltpu.make_async_remote_copy(
            src_ref=src, dst_ref=dst, send_sem=send, recv_sem=recv, device_id=device, device_id_type=MESH
        )

    w_copies = [
        [
            remote(
                weight.at[0, :, columns(k, flip(place[k], e))],
                wv[k].at[rows_of(me)],
                w_s.at[k, e], w_r.at[k, e], (rep, peer[PAIR[k][e]]),
            )
            for e in range(1, GROUP)
        ]
        for k in CLASSES
    ]
    for e in range(GROUP - 1):
        for k in CLASSES:
            w_copies[k][e].start()
    v_copies = [
        [
            remote(
                weight.at[0, :, columns(k, place[k])] if e == 0 else wv[k].at[rows_of(peer[PAIR[k][e]])],
                wv[k].at[rows_of(peer[PAIR[k][e]])],
                v_s.at[k, e], v_r.at[k, e], (rep, peer[TWIN[k]]),
            )
            for e in range(GROUP)
        ]
        for k in CLASSES
    ]
    for k in CLASSES:
        v_copies[k][0].start()

    for i in range(5):
        local[i].wait()
    msg[me, pl.ds(0, TOK), :] = depthv[...].T.astype(BF16)
    spot = jnp.concatenate(
        [
            (idxv[3] * NFRAME + idxv[2]).astype(F32),
            idxv[1].astype(F32),
            idxv[0].astype(F32),
            jnp.zeros((10, 128), F32),
        ],
        axis=0,
    )
    msg[me, pl.ds(TOK, 16), :] = spot.astype(BF16)
    near = [s for s in range(1, SHARE) if s != 6]
    msg_copies = [
        remote(msg.at[me], msg.at[me], msg_s.at[s], msg_r.at[s], (rep, peer[s])) for s in near
    ]
    for copy in msg_copies:
        copy.start()

    def main_copies(c):
        near_ones, far_ones = [], []
        for n, (src, dsts) in enumerate(((tok, tokv), (cot, cotv))):
            for e in (1, 2, 3, 0):
                for k in CLASSES:
                    source = src.at[pl.ds(STARTS[c], SIZES[c]), columns(k, flip(place[k], e))]
                    start = pl.multiple_of(GROUP * STARTS[c] + place[k] * SIZES[c], 32)
                    target = dsts[k].at[pl.ds(start, SIZES[c])]
                    if e == 0:
                        near_ones.append(pltpu.make_async_copy(source, target, main_r.at[c, n, k, 0]))
                    else:
                        far_ones.append(
                            remote(
                                source, target, main_s.at[c, n, k, e], main_r.at[c, n, k, e],
                                (rep, peer[PAIR[k][e]]),
                            )
                        )
        return near_ones, far_ones

    mains = [main_copies(c) for c in range(CHUNKS)]

    def start_main(c):
        for copy in mains[c][1] + mains[c][0]:
            copy.start()

    def start_some(step):
        for n in range(2):
            if ORDER[n][step]:

                @pl.when(core == n)
                def _():
                    for c in ORDER[n][step]:
                        start_main(c)

    start_some(0)

    local[6].wait()
    chosen[...] = fragv[block[0]]
    f_copies = [
        remote(
            chosen.at[pl.ds(mate[s][0] * FP, FP), pl.ds(mate[s][1] * 128, 128)],
            fpart.at[s],
            f_s.at[s], f_r.at[s], (mate_rep(s), me),
        )
        for s in range(1, 16)
    ]
    h_copy = remote(fsum, fother, h_s.at[0], h_r.at[0], (across, me))
    piece = (pl.ds(pl.multiple_of(z * FP, 16), FP), pl.ds(pl.multiple_of(core * 128, 128), 128))
    own = avg.at[piece]
    b_copies = [remote(own, own, b_s.at[s], b_r.at[s], (mate_rep(s), me)) for s in range(1, 16)]

    def scatter():
        @pl.when(me == 0)
        def _():
            pl.semaphore_wait(barrier, 16)
            for s in range(1, SHARE):
                pl.semaphore_signal(crossed, inc=1, device_id=(rep, peer[s]), device_id_type=MESH)

        @pl.when(me != 0)
        def _():
            pl.semaphore_wait(crossed, 1)

        for copy in f_copies:
            copy.start()

    def exchange():
        for copy in f_copies:
            copy.wait_recv()
        total = chosen[piece].astype(F32)
        for s in range(1, 16):
            total = total + fpart[s].astype(F32)
        fsum[...] = total
        h_copy.start()

    def spread_average():
        h_copy.wait_recv()
        avg[piece] = ((fsum[...] + fother[...]) * (1.0 / N_REP)).astype(BF16)
        for copy in b_copies:
            copy.start()

    def nesterov():
        for copy in b_copies:
            copy.wait_recv()
        local[7].wait()
        local[8].wait()

        def body(i, _):
            at = pl.ds(pl.multiple_of(i * 64, 64), 64)
            delta = globv[at, :] - avg[at, :].astype(F32)
            moment = MOMENTUM_RATE * momv[at, :] + delta
            new = globv[at, :] - OUTER_RATE * (MOMENTUM_RATE * moment + delta)
            mom_out[at, :] = moment
            glob_out[at, :] = new
            merged_out[0, at, :] = (
                MIX_RATE * chosen[at, :].astype(F32) + (1.0 - MIX_RATE) * new
            ).astype(BF16)
            return 0

        lax.fori_loop(0, FR // 64, body, 0)

    local[5].wait()
    pixel = lax.broadcasted_iota(jnp.int32, (1, PIX), 1)
    sub_rows = PIX // 16
    horiz = (lax.rem(pixel, 16).astype(F32) + 0.5) / (GW * 16) * 2.0 - 1.0
    vert = ((pixel // 16).astype(F32) + 0.5) / (GH * sub_rows) * 2.0 - 1.0
    table_hi[...] = jnp.zeros_like(table_hi)
    table_lo[...] = jnp.zeros_like(table_lo)

    def put(part, channel, value):
        high = value.astype(BF16)
        where = (pl.ds(part * 128, POSES), pl.ds(channel * PIX, PIX))
        table_hi[where] = high
        table_lo[where] = (value - high.astype(F32)).astype(BF16)

    def entry(k):
        return jnp.broadcast_to(posev[k], (128, POSES)).T

    for ch in range(3):
        first, second, third = entry(3 * ch), entry(3 * ch + 1), entry(3 * ch + 2)
        put(0, ch, first * horiz + second * vert + third)
        put(1, ch, first * (2.0 / GW))
        put(2, ch, second * (2.0 / GH))
        put(0, 3 + ch, entry(9 + ch))

    for e in range(1, GROUP):
        for k in CLASSES:
            w_copies[k][e - 1].wait_recv()
            v_copies[k][e].start()
    start_some(1)

    for copy in msg_copies:
        copy.wait_recv()

    lane = lax.broadcasted_iota(jnp.int32, (128, 128), 1).astype(F32)

    def ray_block(s, _):
        spots = msg[s, pl.ds(TOK, 16), :].astype(F32)
        for half in range(2):
            hot = jnp.where(spread(spots[half : half + 1]) == lane, 1.0, 0.0)
            left = jnp.concatenate(
                [
                    hot,
                    hot * spread(spots[2 + half : 3 + half]),
                    hot * spread(spots[4 + half : 5 + half]),
                ],
                axis=1,
            ).astype(BF16)
            geo = jnp.dot(left, table_hi[...], preferred_element_type=F32) + jnp.dot(
                left, table_lo[...], preferred_element_type=F32
            )
            d = [geo[:, i * PIX : (i + 1) * PIX] for i in range(6)]
            far = msg[s, pl.ds(half * 128, 128), :].astype(F32)
            inv = lax.rsqrt(d[0] * d[0] + d[1] * d[1] + d[2] * d[2])
            close = inv / far
            long = inv * far
            for i in range(6):
                value = d[i] * close if i < 3 else d[i] + d[i - 3] * long
                rays_all[s, pl.ds(half * 128, 128), pl.ds(i * PIX, PIX)] = value.astype(BF16)
        return 0

    def ray_step(n, _):
        return ray_block(lax.rem(me + n, SHARE), 0)

    msg[peer[6]] = msg[me]
    lax.fori_loop(0, SHARE, ray_step, 0)

    for k in CLASSES:
        for i in range(GROUP):
            for c in range(CHUNKS):
                at = GROUP * STARTS[c] + i * SIZES[c]
                rays_t[k][pl.ds(at, SIZES[c]), :] = rays_all[member(k, i), pl.ds(STARTS[c], SIZES[c]), :]

        def turn(b, _, k=k):
            at = pl.ds(pl.multiple_of(b * 128, 128), 128)
            rays[k][:, at] = rays_t[k][at, :].T
            return 0

        lax.fori_loop(0, GT // 128, turn, 0)

    for k in CLASSES:
        w_local[k].wait()
        gain_local[k].wait()
        gacc[k][...] = jnp.zeros_like(gacc[k])
        for copy in v_copies[k]:
            copy.wait_recv()

    wide_lane = lax.broadcasted_iota(jnp.int32, (1, 128), 1)

    def forward(c):
        size = SIZES[c]
        count = 128 // size
        stat[c, 0] = jnp.zeros((SHARE, 128), F32)
        for k in CLASSES:
            for b in range(GROUP * size // 128):
                at = pl.ds(GROUP * STARTS[c] + b * 128, 128)
                lifted = jnp.dot(rays_t[k][at, :], wv[k][...], preferred_element_type=F32)
                hidden = tokv[k][at, :].astype(F32) + lifted
                hid[k][at, :] = hidden
                square = hidden * hidden
                cross = hidden * (cotv[k][at, :].astype(F32) * gainv[k][...])
                q1, q2 = square[:, :128], cross[:, :128]
                for t in range(1, WIDTH[k] // 128):
                    q1 = q1 + square[:, t * 128 : (t + 1) * 128]
                    q2 = q2 + cross[:, t * 128 : (t + 1) * 128]
                r1 = jnp.sum(q1.T, axis=0, keepdims=True)
                r2 = jnp.sum(q2.T, axis=0, keepdims=True)
                for j in range(count):
                    one = pltpu.roll(r1, (128 - j * size) % 128, 1)
                    two = pltpu.roll(r2, (192 - j * size) % 128, 1)
                    source = pl.ds(member(k, b * count + j), 1)
                    stat[c, 0, source, :] += jnp.where(wide_lane < 64, one, two)

    def stat_copies(c):
        return [
            remote(stat.at[c, 0], stat.at[c, s], st_s.at[c, s], st_r.at[c, s], (rep, peer[s]))
            for s in range(1, SHARE)
        ]

    def backward(c):
        size = SIZES[c]
        count = 128 // size
        both = stat[c, 0]
        for s in range(1, SHARE):
            both = both + stat[c, s]
        scale = lax.rsqrt(both / D + EPS)
        scales[...] = scale
        pulls[...] = scale * scale * scale * (pltpu.roll(both, 64, 1) / D)

        def gather(ref, k, b):
            row = ref[pl.ds(member(k, b * count), 1), :]
            for j in range(1, count):
                other = pltpu.roll(ref[pl.ds(member(k, b * count + j), 1), :], j * size, 1)
                row = jnp.where(wide_lane < j * size, row, other)
            return spread(row)

        for k in CLASSES:
            for b in range(GROUP * size // 128):
                wide = gather(scales, k, b)
                wide_pull = gather(pulls, k, b)
                at = pl.ds(GROUP * STARTS[c] + b * 128, 128)
                for t in range(WIDTH[k] // 128):
                    cols = pl.ds(t * 128, 128)
                    hidden = hid[k][at, cols]
                    up = cotv[k][at, cols].astype(F32) * wide
                    slope[k][pl.ds(b * 128, 128), cols] = (
                        up * gainv[k][:, cols] - wide_pull * hidden
                    ).astype(BF16)
                    prod = up * hidden
                    part_sum = prod[0:8]
                    for i in range(1, 16):
                        part_sum = part_sum + prod[i * 8 : (i + 1) * 8]
                    gacc[k][:, cols] += part_sum

    def product(c, k, at):
        count = GROUP * SIZES[c]
        return jnp.dot(
            rays[k][at, pl.ds(GROUP * STARTS[c], count)],
            slope[k][pl.ds(0, count), :],
            preferred_element_type=F32,
        )

    def spend(c):
        for k in CLASSES:

            def body(i, _, k=k):
                at = pl.ds(pl.multiple_of(i * 192, 192), 192)
                if c == 0:
                    acc[k][at, :] = product(c, k, at)
                else:
                    acc[k][at, :] += product(c, k, at)
                return 0

            lax.fori_loop(0, PIN // 192, body, 0)

    stats = [stat_copies(c) for c in range(CHUNKS)]
    for c in range(CHUNKS):
        for copy in mains[c][1]:
            copy.wait_recv()
        for copy in mains[c][0]:
            copy.wait()
        for copy in mains[c][1]:
            copy.wait_send()
        start_some(c + 2)
        forward(c)
        for copy in stats[c]:
            copy.start()
        if c == 0:
            scatter()
        if c == 1:
            exchange()
        if c == 2:
            spread_average()
        if c > 0:
            for copy in stats[c - 1]:
                copy.wait_recv()
            backward(c - 1)
            spend(c - 1)
    last = CHUNKS - 1
    for copy in stats[last]:
        copy.wait_recv()
    backward(last)

    p_copies = {}
    for e in (1, 2, 3, 0):
        for k in CLASSES:
            at = rows_of(peer[TWIN[k] ^ PAIR[k][e]])
            send[k][e] = (acc[k][at, :] + product(last, k, at)).astype(BF16)
            copy = remote(send[k].at[e], part[k].at[e], p_s.at[k, e], p_r.at[k, e], (rep, peer[TWIN[k]]))
            copy.start()
            p_copies[k, e] = copy
    for k in CLASSES:
        for t in range(WIDTH[k] // 128):
            n = sum(WIDTH[:k]) // 128 + t
            gains[me, pl.ds(n, 1), :] = jnp.sum(gacc[k][:, pl.ds(t * 128, 128)], axis=0, keepdims=True)
    gain_copies = [
        remote(gains.at[me], gains.at[me], gg_s.at[s], gg_r.at[s], (rep, peer[s])) for s in range(1, SHARE)
    ]
    for copy in gain_copies:
        copy.start()
    g_copies = []
    for e in (1, 2, 3, 0):
        for k in CLASSES:
            at = rows_of(peer[PAIR[k][e]])
            value = acc[k][at, :] + product(last, k, at)
            p_copies[k, e].wait_recv()
            value = (value + part[k][e].astype(F32)).astype(BF16)
            if e == 0:
                grad_out[0, :, columns(k, place[k])] = value
            else:
                last_out[k][e - 1] = value
                copy = remote(
                    last_out[k].at[e - 1], grad_out.at[0, :, columns(k, place[k])],
                    g_s.at[k, e], g_r.at[k, e], (rep, peer[PAIR[k][e]]),
                )
                copy.start()
                g_copies.append(copy)
    nesterov()
    for copy in gain_copies:
        copy.wait_recv()
    seen = set()
    for s in range(SHARE):
        for n in range(10):
            tile = pl.ds(gain_tile(s, n), 1)
            value = gains[s, pl.ds(n, 1), :]
            gsum[tile, :] = gsum[tile, :] + value if gain_tile(s, n) in seen else value
            seen.add(gain_tile(s, n))
    for t in range(DS // 128):
        gain_out[:, pl.ds(t * 128, 128)] = gsum[pl.ds(me * (DS // 128) + t, 1), :]

    for k in CLASSES:
        for copy in w_copies[k] + v_copies[k]:
            copy.wait_send()
    for copy in msg_copies + list(p_copies.values()) + gain_copies + f_copies + [h_copy] + b_copies:
        copy.wait_send()
    for c in range(CHUNKS):
        for copy in stats[c]:
            copy.wait_send()
    for copy in g_copies:
        copy.wait()


def finish(*refs):
    ins, outs, sem = refs[:5], refs[5:10], refs[10]
    copies = [pltpu.make_async_copy(a, b, sem.at[i]) for i, (a, b) in enumerate(zip(ins, outs))]
    for copy in copies:
        copy.start()
    for copy in copies:
        copy.wait()


def shards(
    tokens, cotangent, token_row, token_col, token_frame, token_camera, pixel_depth,
    cam_poses, cam_weight, gain, frag_stack, frag_block, global_frag, momentum,
):
    dma = pltpu.SemaphoreType.DMA
    hbm = pl.BlockSpec(memory_space=pltpu.HBM)
    places = [a.reshape(2, 128) for a in (token_row, token_col, token_frame, token_camera)]
    shapes = (((1, ROWS, D), BF16), ((1, DS), F32), ((FR, 256), F32), ((FR, 256), F32), ((1, FR, 256), BF16))
    results = pl.pallas_call(
        kernel,
        name="step",
        out_shape=tuple(pltpu.VMEM(*one) for one in shapes),
        in_specs=[hbm] * 11 + [pl.BlockSpec(memory_space=pltpu.SMEM)] + [hbm] * 2,
        out_specs=(pl.BlockSpec(memory_space=pltpu.VMEM),) * 5,
        scratch_shapes=[
            *[pltpu.VMEM((GT, w), BF16) for w in WIDTH],
            *[pltpu.VMEM((GT, w), BF16) for w in WIDTH],
            *[pltpu.VMEM((PIN, w), BF16) for w in WIDTH],
            *[pltpu.VMEM((GT, PIN), BF16) for w in WIDTH],
            *[pltpu.VMEM((PIN, GT), BF16) for w in WIDTH],
            *[pltpu.VMEM((GT, w), F32) for w in WIDTH],
            *[pltpu.VMEM((GROUP * max(SIZES), w), BF16) for w in WIDTH],
            *[pltpu.VMEM((PIN, w), F32) for w in WIDTH],
            *[pltpu.VMEM((GROUP, ROWS, w), BF16) for w in WIDTH],
            *[pltpu.VMEM((GROUP, ROWS, w), BF16) for w in WIDTH],
            *[pltpu.VMEM((GROUP - 1, ROWS, w), BF16) for w in WIDTH],
            *[pltpu.VMEM((8, w), F32) for w in WIDTH],
            *[pltpu.VMEM((1, w), F32) for w in WIDTH],
            pltpu.VMEM((SHARE, MSG, 128), BF16),
            pltpu.VMEM((PIX, TOK), F32),
            pltpu.VMEM((4, 2, 128), jnp.int32),
            pltpu.VMEM((12, 1, POSES), F32),
            pltpu.VMEM((384, PIN), BF16),
            pltpu.VMEM((384, PIN), BF16),
            pltpu.VMEM((SHARE, TOK, PIN), BF16),
            pltpu.VMEM((CHUNKS, SHARE, SHARE, 128), F32),
            pltpu.VMEM((SHARE, 128), F32),
            pltpu.VMEM((SHARE, 128), F32),
            pltpu.VMEM((SHARE, 16, 128), F32),
            pltpu.VMEM((D // 128, 128), F32),
            pltpu.VMEM((6, FR, 256), BF16),
            pltpu.VMEM((FR, 256), BF16),
            pltpu.VMEM((16, FP, 128), BF16),
            pltpu.VMEM((FP, 128), F32),
            pltpu.VMEM((FP, 128), F32),
            pltpu.VMEM((FR, 256), BF16),
            pltpu.VMEM((FR, 256), F32),
            pltpu.VMEM((FR, 256), F32),
            dma((9,)), dma((3,)), dma((3,)),
            dma((CHUNKS, 2, 3, GROUP)), dma((CHUNKS, 2, 3, GROUP)),
            dma((3, GROUP)), dma((3, GROUP)),
            dma((3, GROUP)), dma((3, GROUP)),
            dma((SHARE,)), dma((SHARE,)),
            dma((CHUNKS, SHARE)), dma((CHUNKS, SHARE)),
            dma((3, GROUP)), dma((3, GROUP)),
            dma((3, GROUP)), dma((3, GROUP)),
            dma((SHARE,)), dma((SHARE,)),
            dma((16,)), dma((16,)),
            dma((1,)), dma((1,)),
            dma((16,)), dma((16,)),
            pltpu.SemaphoreType.REGULAR, pltpu.SemaphoreType.REGULAR,
        ],
        compiler_params=pltpu.CompilerParams(
            collective_id=0, has_side_effects=True, vmem_limit_bytes=56 << 20
        ),
        cost_estimate=pl.CostEstimate(flops=6 << 30, bytes_accessed=20 << 20, transcendentals=0),
    )(
        *[
            pltpu.with_memory_space_constraint(a, pltpu.HBM)
            for a in (
                tokens, cotangent, *places, pixel_depth, cam_poses.transpose(1, 0, 2), cam_weight, gain, frag_stack
            )
        ],
        *[pltpu.with_memory_space_constraint(a, pltpu.HBM) for a in (frag_block, global_frag, momentum)],
    )
    return pl.pallas_call(
        finish,
        name="finish",
        out_shape=tuple(jax.ShapeDtypeStruct(*one) for one in shapes),
        in_specs=[pl.BlockSpec(memory_space=pltpu.VMEM)] * 5,
        out_specs=(pl.BlockSpec(memory_space=pltpu.HBM),) * 5,
        scratch_shapes=[dma((5,))],
    )(*[pltpu.with_memory_space_constraint(a, pltpu.VMEM) for a in results])


def solution(mesh):
    placed = (
        P(("rep", "fsdp"), None),
        P(("rep", "fsdp"), None),
        P(("rep", "fsdp")),
        P(("rep", "fsdp")),
        P(("rep", "fsdp")),
        P(("rep", "fsdp")),
        P(None, ("rep", "fsdp")),
        P("rep", None, None),
        P("rep", "fsdp", None),
        P("rep", None),
        P("rep", None, "fsdp", None),
        P(),
        P("fsdp", None),
        P("fsdp", None),
    )
    return jax.shard_map(
        shards,
        mesh=mesh,
        in_specs=placed,
        out_specs=(
            P("rep", "fsdp", None),
            P("rep", "fsdp"),
            P("fsdp", None),
            P("fsdp", None),
            P("rep", "fsdp", None),
        ),
        check_vma=False,
    )
```

```python
import jax
import jax.numpy as jnp
from jax import lax
from jax.experimental import pallas as pl
from jax.experimental.pallas import tpu as pltpu
from jax.sharding import PartitionSpec as P

D = 5120
PIX = 128
NFRAME = 24
GH = 44
GW = 80
PIN = 768
POSES = 96
N_REP = 32
SHARE = 8
DS = D // SHARE
ROWS = PIN // SHARE
TOK = 256
FR = 640
FP = 80
MSG = TOK + 16

WIDTH = (512, 384, 384)
BASE = (0, 2048, 3584)
PAIR = ((0, 1, 2, 3), (0, 1, 4, 5), (0, 3, 4, 7))
TWIN = (4, 3, 1)
CLASSES = range(3)
GROUP = 4
GT = GROUP * TOK

SIZES = (64, 64, 64, 64)
STARTS = tuple(sum(SIZES[:c]) for c in range(len(SIZES)))
CHUNKS = len(SIZES)
ORDER = (((0,), (), (1,), (2, 3), (), ()), ((0,), (1, 2), (3,), (), (), ()))

EPS = 1e-06
MOMENTUM_RATE = 0.9
OUTER_RATE = 0.7
MIX_RATE = 0.5

MESH = pl.DeviceIdType.MESH
F32 = jnp.float32
BF16 = jnp.bfloat16


def spread(row):
    return jnp.broadcast_to(row, (128, 128)).T


def flip(a, b):
    out = a
    for i in range(3):
        if b >> i & 1:
            out = out + (1 << i) * (1 - 2 * lax.rem(a // (1 << i), 2))
    return out


def gain_tile(device, place):
    x, y = device // 4, device % 4
    slots = (y, x * 2 + ((y >> 1 ^ y) & 1), x * 2 + (y >> 1))
    for k in CLASSES:
        tiles = WIDTH[k] // 128
        if place < tiles:
            return BASE[k] // 128 + slots[k] * tiles + place
        place -= tiles


def kernel(
    tok, cot, trow, tcol, tfr, tcam, depth, poses, weight, gain, frag, block, glob, mom,
    grad_out, gain_out, glob_out, mom_out, merged_out,
    tok_a, tok_b, tok_c, cot_a, cot_b, cot_c, w_a, w_b, w_c, rt_a, rt_b, rt_c, rays_a, rays_b, rays_c,
    hid_a, hid_b, hid_c, slope_a, slope_b, slope_c, acc_a, acc_b, acc_c, send_a, send_b, send_c,
    part_a, part_b, part_c, last_a, last_b, last_c, gacc_a, gacc_b, gacc_c, gain_a, gain_b, gain_c,
    msg, depthv, idxv, posev, table_hi, table_lo, rays_all, stat, scales, pulls, gains, gsum,
    fragv, chosen, fpart, fsum, fother, avg, globv, momv,
    lsem, wl_s, gl_s, main_s, main_r, w_s, w_r, v_s, v_r, msg_s, msg_r, st_s, st_r, p_s, p_r, g_s, g_r,
    gg_s, gg_r, f_s, f_r, h_s, h_r, b_s, b_r, ready, crossed,
):
    tokv, cotv, wv = (tok_a, tok_b, tok_c), (cot_a, cot_b, cot_c), (w_a, w_b, w_c)
    rays_t, rays, hid = (rt_a, rt_b, rt_c), (rays_a, rays_b, rays_c), (hid_a, hid_b, hid_c)
    slope, acc, send = (slope_a, slope_b, slope_c), (acc_a, acc_b, acc_c), (send_a, send_b, send_c)
    part, last_out, gacc = (part_a, part_b, part_c), (last_a, last_b, last_c), (gacc_a, gacc_b, gacc_c)
    gainv = (gain_a, gain_b, gain_c)

    rep, me = lax.axis_index("rep"), lax.axis_index("fsdp")
    z, xh, core = rep // 4, lax.rem(rep // 2, 2), lax.rem(rep, 2)
    x, y = me // 4, lax.rem(me, 4)
    high, low = y // 2, lax.rem(y, 2)
    odd = high + low - 2 * high * low
    peer = [flip(me, s) for s in range(SHARE)]
    place = (y, x * 2 + odd, x * 2 + high)

    def member(k, i):
        if k == 0:
            return x * 4 + i
        s = i & 1
        if k == 1:
            return (i >> 1) * 4 + 2 * high + (1 - high if s else high)
        return (i >> 1) * 4 + 2 * s + (1 - odd if s else odd)

    def columns(k, at):
        return pl.ds(pl.multiple_of(BASE[k] + at * WIDTH[k], 128), WIDTH[k])

    def rows_of(device):
        return pl.ds(pl.multiple_of(device * ROWS, 32), ROWS)

    mate = [(flip(z, s >> 1), flip(core, s & 1)) for s in range(16)]

    def mate_rep(s):
        return mate[s][0] * 4 + xh * 2 + mate[s][1]

    across = z * 4 + (1 - xh) * 2 + core

    barrier = pltpu.get_barrier_semaphore()
    for s in range(1, SHARE):

        @pl.when(peer[s] != 0)
        def _():
            pl.semaphore_signal(barrier, inc=1, device_id=(rep, peer[s]), device_id_type=MESH)

    local = [
        pltpu.make_async_copy(depth, depthv, lsem.at[0]),
        pltpu.make_async_copy(trow, idxv.at[0], lsem.at[1]),
        pltpu.make_async_copy(tcol, idxv.at[1], lsem.at[2]),
        pltpu.make_async_copy(tfr, idxv.at[2], lsem.at[3]),
        pltpu.make_async_copy(tcam, idxv.at[3], lsem.at[4]),
        pltpu.make_async_copy(poses, posev, lsem.at[5]),
        pltpu.make_async_copy(frag.at[0], fragv, lsem.at[6]),
        pltpu.make_async_copy(glob, globv, lsem.at[7]),
        pltpu.make_async_copy(mom, momv, lsem.at[8]),
    ]
    for copy in local:
        copy.start()
    w_local = [
        pltpu.make_async_copy(weight.at[0, :, columns(k, place[k])], wv[k].at[rows_of(me)], wl_s.at[k])
        for k in CLASSES
    ]
    gain_local = [
        pltpu.make_async_copy(gain.at[:, columns(k, place[k])], gainv[k], gl_s.at[k]) for k in CLASSES
    ]
    for copy in w_local + gain_local:
        copy.start()

    @pl.when(me != 0)
    def _():
        pl.semaphore_wait(barrier, SHARE - 1)
        pl.semaphore_signal(ready, inc=1, device_id=(rep, 0), device_id_type=MESH)

    @pl.when(me == 0)
    def _():
        pl.semaphore_wait(ready, SHARE - 1)
        for s in range(1, 16):
            pl.semaphore_signal(barrier, inc=1, device_id=(mate_rep(s), me), device_id_type=MESH)
        pl.semaphore_signal(barrier, inc=1, device_id=(across, me), device_id_type=MESH)

    def remote(src, dst, send, recv, device):
        return pltpu.make_async_remote_copy(
            src_ref=src, dst_ref=dst, send_sem=send, recv_sem=recv, device_id=device, device_id_type=MESH
        )

    w_copies = [
        [
            remote(
                weight.at[0, :, columns(k, flip(place[k], e))],
                wv[k].at[rows_of(me)],
                w_s.at[k, e], w_r.at[k, e], (rep, peer[PAIR[k][e]]),
            )
            for e in range(1, GROUP)
        ]
        for k in CLASSES
    ]
    for e in range(GROUP - 1):
        for k in CLASSES:
            w_copies[k][e].start()
    v_copies = [
        [
            remote(
                weight.at[0, :, columns(k, place[k])] if e == 0 else wv[k].at[rows_of(peer[PAIR[k][e]])],
                wv[k].at[rows_of(peer[PAIR[k][e]])],
                v_s.at[k, e], v_r.at[k, e], (rep, peer[TWIN[k]]),
            )
            for e in range(GROUP)
        ]
        for k in CLASSES
    ]
    for k in CLASSES:
        v_copies[k][0].start()

    for i in range(5):
        local[i].wait()
    msg[me, pl.ds(0, TOK), :] = depthv[...].T.astype(BF16)
    spot = jnp.concatenate(
        [
            (idxv[3] * NFRAME + idxv[2]).astype(F32),
            idxv[1].astype(F32),
            idxv[0].astype(F32),
            jnp.zeros((10, 128), F32),
        ],
        axis=0,
    )
    msg[me, pl.ds(TOK, 16), :] = spot.astype(BF16)
    near = [s for s in range(1, SHARE) if s != 6]
    msg_copies = [
        remote(msg.at[me], msg.at[me], msg_s.at[s], msg_r.at[s], (rep, peer[s])) for s in near
    ]
    for copy in msg_copies:
        copy.start()

    def main_copies(c):
        near_ones, far_ones = [], []
        for n, (src, dsts) in enumerate(((tok, tokv), (cot, cotv))):
            for e in (1, 2, 3, 0):
                for k in CLASSES:
                    source = src.at[pl.ds(STARTS[c], SIZES[c]), columns(k, flip(place[k], e))]
                    start = pl.multiple_of(GROUP * STARTS[c] + place[k] * SIZES[c], 32)
                    target = dsts[k].at[pl.ds(start, SIZES[c])]
                    if e == 0:
                        near_ones.append(pltpu.make_async_copy(source, target, main_r.at[c, n, k, 0]))
                    else:
                        far_ones.append(
                            remote(
                                source, target, main_s.at[c, n, k, e], main_r.at[c, n, k, e],
                                (rep, peer[PAIR[k][e]]),
                            )
                        )
        return near_ones, far_ones

    mains = [main_copies(c) for c in range(CHUNKS)]

    def start_main(c):
        for copy in mains[c][1] + mains[c][0]:
            copy.start()

    def start_some(step):
        for n in range(2):
            if ORDER[n][step]:

                @pl.when(core == n)
                def _():
                    for c in ORDER[n][step]:
                        start_main(c)

    start_some(0)

    local[6].wait()
    chosen[...] = fragv[block[0]]
    f_copies = [
        remote(
            chosen.at[pl.ds(mate[s][0] * FP, FP), pl.ds(mate[s][1] * 128, 128)],
            fpart.at[s],
            f_s.at[s], f_r.at[s], (mate_rep(s), me),
        )
        for s in range(1, 16)
    ]
    h_copy = remote(fsum, fother, h_s.at[0], h_r.at[0], (across, me))
    piece = (pl.ds(pl.multiple_of(z * FP, 16), FP), pl.ds(pl.multiple_of(core * 128, 128), 128))
    own = avg.at[piece]
    b_copies = [remote(own, own, b_s.at[s], b_r.at[s], (mate_rep(s), me)) for s in range(1, 16)]

    def scatter():
        @pl.when(me == 0)
        def _():
            pl.semaphore_wait(barrier, 16)
            for s in range(1, SHARE):
                pl.semaphore_signal(crossed, inc=1, device_id=(rep, peer[s]), device_id_type=MESH)

        @pl.when(me != 0)
        def _():
            pl.semaphore_wait(crossed, 1)

        for copy in f_copies:
            copy.start()

    def exchange():
        for copy in f_copies:
            copy.wait_recv()
        total = chosen[piece].astype(F32)
        for s in range(1, 16):
            total = total + fpart[s].astype(F32)
        fsum[...] = total
        h_copy.start()

    def spread_average():
        h_copy.wait_recv()
        avg[piece] = ((fsum[...] + fother[...]) * (1.0 / N_REP)).astype(BF16)
        for copy in b_copies:
            copy.start()

    def nesterov():
        for copy in b_copies:
            copy.wait_recv()
        local[7].wait()
        local[8].wait()

        def body(i, _):
            at = pl.ds(pl.multiple_of(i * 64, 64), 64)
            delta = globv[at, :] - avg[at, :].astype(F32)
            moment = MOMENTUM_RATE * momv[at, :] + delta
            new = globv[at, :] - OUTER_RATE * (MOMENTUM_RATE * moment + delta)
            mom_out[at, :] = moment
            glob_out[at, :] = new
            merged_out[0, at, :] = (
                MIX_RATE * chosen[at, :].astype(F32) + (1.0 - MIX_RATE) * new
            ).astype(BF16)
            return 0

        lax.fori_loop(0, FR // 64, body, 0)

    local[5].wait()
    pixel = lax.broadcasted_iota(jnp.int32, (1, PIX), 1)
    sub_rows = PIX // 16
    horiz = (lax.rem(pixel, 16).astype(F32) + 0.5) / (GW * 16) * 2.0 - 1.0
    vert = ((pixel // 16).astype(F32) + 0.5) / (GH * sub_rows) * 2.0 - 1.0
    table_hi[...] = jnp.zeros_like(table_hi)
    table_lo[...] = jnp.zeros_like(table_lo)

    def put(part, channel, value):
        high = value.astype(BF16)
        where = (pl.ds(part * 128, POSES), pl.ds(channel * PIX, PIX))
        table_hi[where] = high
        table_lo[where] = (value - high.astype(F32)).astype(BF16)

    def entry(k):
        return jnp.broadcast_to(posev[k], (128, POSES)).T

    for ch in range(3):
        first, second, third = entry(3 * ch), entry(3 * ch + 1), entry(3 * ch + 2)
        put(0, ch, first * horiz + second * vert + third)
        put(1, ch, first * (2.0 / GW))
        put(2, ch, second * (2.0 / GH))
        put(0, 3 + ch, entry(9 + ch))

    for e in range(1, GROUP):
        for k in CLASSES:
            w_copies[k][e - 1].wait_recv()
            v_copies[k][e].start()
    start_some(1)

    for copy in msg_copies:
        copy.wait_recv()

    lane = lax.broadcasted_iota(jnp.int32, (128, 128), 1).astype(F32)

    def ray_block(s, _):
        spots = msg[s, pl.ds(TOK, 16), :].astype(F32)
        for half in range(2):
            hot = jnp.where(spread(spots[half : half + 1]) == lane, 1.0, 0.0)
            left = jnp.concatenate(
                [
                    hot,
                    hot * spread(spots[2 + half : 3 + half]),
                    hot * spread(spots[4 + half : 5 + half]),
                ],
                axis=1,
            ).astype(BF16)
            geo = jnp.dot(left, table_hi[...], preferred_element_type=F32) + jnp.dot(
                left, table_lo[...], preferred_element_type=F32
            )
            d = [geo[:, i * PIX : (i + 1) * PIX] for i in range(6)]
            far = msg[s, pl.ds(half * 128, 128), :].astype(F32)
            inv = lax.rsqrt(d[0] * d[0] + d[1] * d[1] + d[2] * d[2])
            close = inv / far
            long = inv * far
            for i in range(6):
                value = d[i] * close if i < 3 else d[i] + d[i - 3] * long
                rays_all[s, pl.ds(half * 128, 128), pl.ds(i * PIX, PIX)] = value.astype(BF16)
        return 0

    def ray_step(n, _):
        return ray_block(lax.rem(me + n, SHARE), 0)

    msg[peer[6]] = msg[me]
    lax.fori_loop(0, SHARE, ray_step, 0)

    for k in CLASSES:
        for i in range(GROUP):
            for c in range(CHUNKS):
                at = GROUP * STARTS[c] + i * SIZES[c]
                rays_t[k][pl.ds(at, SIZES[c]), :] = rays_all[member(k, i), pl.ds(STARTS[c], SIZES[c]), :]

        def turn(b, _, k=k):
            at = pl.ds(pl.multiple_of(b * 128, 128), 128)
            rays[k][:, at] = rays_t[k][at, :].T
            return 0

        lax.fori_loop(0, GT // 128, turn, 0)

    for k in CLASSES:
        w_local[k].wait()
        gain_local[k].wait()
        gacc[k][...] = jnp.zeros_like(gacc[k])
        for copy in v_copies[k]:
            copy.wait_recv()

    wide_lane = lax.broadcasted_iota(jnp.int32, (1, 128), 1)

    def forward(c):
        size = SIZES[c]
        count = 128 // size
        stat[c, 0] = jnp.zeros((SHARE, 128), F32)
        for k in CLASSES:
            for b in range(GROUP * size // 128):
                at = pl.ds(GROUP * STARTS[c] + b * 128, 128)
                lifted = jnp.dot(rays_t[k][at, :], wv[k][...], preferred_element_type=F32)
                hidden = tokv[k][at, :].astype(F32) + lifted
                hid[k][at, :] = hidden
                square = hidden * hidden
                cross = hidden * (cotv[k][at, :].astype(F32) * gainv[k][...])
                q1, q2 = square[:, :128], cross[:, :128]
                for t in range(1, WIDTH[k] // 128):
                    q1 = q1 + square[:, t * 128 : (t + 1) * 128]
                    q2 = q2 + cross[:, t * 128 : (t + 1) * 128]
                r1 = jnp.sum(q1.T, axis=0, keepdims=True)
                r2 = jnp.sum(q2.T, axis=0, keepdims=True)
                for j in range(count):
                    one = pltpu.roll(r1, (128 - j * size) % 128, 1)
                    two = pltpu.roll(r2, (192 - j * size) % 128, 1)
                    source = pl.ds(member(k, b * count + j), 1)
                    stat[c, 0, source, :] += jnp.where(wide_lane < 64, one, two)

    def stat_copies(c):
        return [
            remote(stat.at[c, 0], stat.at[c, s], st_s.at[c, s], st_r.at[c, s], (rep, peer[s]))
            for s in range(1, SHARE)
        ]

    def backward(c):
        size = SIZES[c]
        count = 128 // size
        both = stat[c, 0]
        for s in range(1, SHARE):
            both = both + stat[c, s]
        scale = lax.rsqrt(both / D + EPS)
        scales[...] = scale
        pulls[...] = scale * scale * scale * (pltpu.roll(both, 64, 1) / D)

        def gather(ref, k, b):
            row = ref[pl.ds(member(k, b * count), 1), :]
            for j in range(1, count):
                other = pltpu.roll(ref[pl.ds(member(k, b * count + j), 1), :], j * size, 1)
                row = jnp.where(wide_lane < j * size, row, other)
            return spread(row)

        for k in CLASSES:
            for b in range(GROUP * size // 128):
                wide = gather(scales, k, b)
                wide_pull = gather(pulls, k, b)
                at = pl.ds(GROUP * STARTS[c] + b * 128, 128)
                for t in range(WIDTH[k] // 128):
                    cols = pl.ds(t * 128, 128)
                    hidden = hid[k][at, cols]
                    up = cotv[k][at, cols].astype(F32) * wide
                    slope[k][pl.ds(b * 128, 128), cols] = (
                        up * gainv[k][:, cols] - wide_pull * hidden
                    ).astype(BF16)
                    prod = up * hidden
                    part_sum = prod[0:8]
                    for i in range(1, 16):
                        part_sum = part_sum + prod[i * 8 : (i + 1) * 8]
                    gacc[k][:, cols] += part_sum

    def product(c, k, at):
        count = GROUP * SIZES[c]
        return jnp.dot(
            rays[k][at, pl.ds(GROUP * STARTS[c], count)],
            slope[k][pl.ds(0, count), :],
            preferred_element_type=F32,
        )

    def spend(c):
        for k in CLASSES:

            def body(i, _, k=k):
                at = pl.ds(pl.multiple_of(i * 192, 192), 192)
                if c == 0:
                    acc[k][at, :] = product(c, k, at)
                else:
                    acc[k][at, :] += product(c, k, at)
                return 0

            lax.fori_loop(0, PIN // 192, body, 0)

    stats = [stat_copies(c) for c in range(CHUNKS)]
    for c in range(CHUNKS):
        for copy in mains[c][1]:
            copy.wait_recv()
        for copy in mains[c][0]:
            copy.wait()
        for copy in mains[c][1]:
            copy.wait_send()
        start_some(c + 2)
        forward(c)
        for copy in stats[c]:
            copy.start()
        if c == 0:
            scatter()
        if c == 1:
            exchange()
        if c == 2:
            spread_average()
        if c > 0:
            for copy in stats[c - 1]:
                copy.wait_recv()
            backward(c - 1)
            spend(c - 1)
    last = CHUNKS - 1
    for copy in stats[last]:
        copy.wait_recv()
    backward(last)

    p_copies = {}
    for e in (1, 2, 3, 0):
        for k in CLASSES:
            at = rows_of(peer[TWIN[k] ^ PAIR[k][e]])
            send[k][e] = (acc[k][at, :] + product(last, k, at)).astype(BF16)
            copy = remote(send[k].at[e], part[k].at[e], p_s.at[k, e], p_r.at[k, e], (rep, peer[TWIN[k]]))
            copy.start()
            p_copies[k, e] = copy
    for k in CLASSES:
        for t in range(WIDTH[k] // 128):
            n = sum(WIDTH[:k]) // 128 + t
            gains[me, pl.ds(n, 1), :] = jnp.sum(gacc[k][:, pl.ds(t * 128, 128)], axis=0, keepdims=True)
    gain_copies = [
        remote(gains.at[me], gains.at[me], gg_s.at[s], gg_r.at[s], (rep, peer[s])) for s in range(1, SHARE)
    ]
    for copy in gain_copies:
        copy.start()
    g_copies = []
    for e in (1, 2, 3, 0):
        for k in CLASSES:
            at = rows_of(peer[PAIR[k][e]])
            value = acc[k][at, :] + product(last, k, at)
            p_copies[k, e].wait_recv()
            value = (value + part[k][e].astype(F32)).astype(BF16)
            if e == 0:
                grad_out[0, :, columns(k, place[k])] = value
            else:
                last_out[k][e - 1] = value
                copy = remote(
                    last_out[k].at[e - 1], grad_out.at[0, :, columns(k, place[k])],
                    g_s.at[k, e], g_r.at[k, e], (rep, peer[PAIR[k][e]]),
                )
                copy.start()
                g_copies.append(copy)
    nesterov()
    for copy in gain_copies:
        copy.wait_recv()
    seen = set()
    for s in range(SHARE):
        for n in range(10):
            tile = pl.ds(gain_tile(s, n), 1)
            value = gains[s, pl.ds(n, 1), :]
            gsum[tile, :] = gsum[tile, :] + value if gain_tile(s, n) in seen else value
            seen.add(gain_tile(s, n))
    for t in range(DS // 128):
        gain_out[:, pl.ds(t * 128, 128)] = gsum[pl.ds(me * (DS // 128) + t, 1), :]

    for k in CLASSES:
        for copy in w_copies[k] + v_copies[k]:
            copy.wait_send()
    for copy in msg_copies + list(p_copies.values()) + gain_copies + f_copies + [h_copy] + b_copies:
        copy.wait_send()
    for c in range(CHUNKS):
        for copy in stats[c]:
            copy.wait_send()
    for copy in g_copies:
        copy.wait()


def finish(*refs):
    ins, outs, sem = refs[:5], refs[5:10], refs[10]
    copies = [pltpu.make_async_copy(a, b, sem.at[i]) for i, (a, b) in enumerate(zip(ins, outs))]
    for copy in copies:
        copy.start()
    for copy in copies:
        copy.wait()


def shards(
    tokens, cotangent, token_row, token_col, token_frame, token_camera, pixel_depth,
    cam_poses, cam_weight, gain, frag_stack, frag_block, global_frag, momentum,
):
    dma = pltpu.SemaphoreType.DMA
    hbm = pl.BlockSpec(memory_space=pltpu.HBM)
    places = [a.reshape(2, 128) for a in (token_row, token_col, token_frame, token_camera)]
    shapes = (((1, ROWS, D), BF16), ((1, DS), F32), ((FR, 256), F32), ((FR, 256), F32), ((1, FR, 256), BF16))
    results = pl.pallas_call(
        kernel,
        name="step",
        out_shape=tuple(pltpu.VMEM(*one) for one in shapes),
        in_specs=[hbm] * 11 + [pl.BlockSpec(memory_space=pltpu.SMEM)] + [hbm] * 2,
        out_specs=(pl.BlockSpec(memory_space=pltpu.VMEM),) * 5,
        scratch_shapes=[
            *[pltpu.VMEM((GT, w), BF16) for w in WIDTH],
            *[pltpu.VMEM((GT, w), BF16) for w in WIDTH],
            *[pltpu.VMEM((PIN, w), BF16) for w in WIDTH],
            *[pltpu.VMEM((GT, PIN), BF16) for w in WIDTH],
            *[pltpu.VMEM((PIN, GT), BF16) for w in WIDTH],
            *[pltpu.VMEM((GT, w), F32) for w in WIDTH],
            *[pltpu.VMEM((GROUP * max(SIZES), w), BF16) for w in WIDTH],
            *[pltpu.VMEM((PIN, w), F32) for w in WIDTH],
            *[pltpu.VMEM((GROUP, ROWS, w), BF16) for w in WIDTH],
            *[pltpu.VMEM((GROUP, ROWS, w), BF16) for w in WIDTH],
            *[pltpu.VMEM((GROUP - 1, ROWS, w), BF16) for w in WIDTH],
            *[pltpu.VMEM((8, w), F32) for w in WIDTH],
            *[pltpu.VMEM((1, w), F32) for w in WIDTH],
            pltpu.VMEM((SHARE, MSG, 128), BF16),
            pltpu.VMEM((PIX, TOK), F32),
            pltpu.VMEM((4, 2, 128), jnp.int32),
            pltpu.VMEM((12, 1, POSES), F32),
            pltpu.VMEM((384, PIN), BF16),
            pltpu.VMEM((384, PIN), BF16),
            pltpu.VMEM((SHARE, TOK, PIN), BF16),
            pltpu.VMEM((CHUNKS, SHARE, SHARE, 128), F32),
            pltpu.VMEM((SHARE, 128), F32),
            pltpu.VMEM((SHARE, 128), F32),
            pltpu.VMEM((SHARE, 16, 128), F32),
            pltpu.VMEM((D // 128, 128), F32),
            pltpu.VMEM((6, FR, 256), BF16),
            pltpu.VMEM((FR, 256), BF16),
            pltpu.VMEM((16, FP, 128), BF16),
            pltpu.VMEM((FP, 128), F32),
            pltpu.VMEM((FP, 128), F32),
            pltpu.VMEM((FR, 256), BF16),
            pltpu.VMEM((FR, 256), F32),
            pltpu.VMEM((FR, 256), F32),
            dma((9,)), dma((3,)), dma((3,)),
            dma((CHUNKS, 2, 3, GROUP)), dma((CHUNKS, 2, 3, GROUP)),
            dma((3, GROUP)), dma((3, GROUP)),
            dma((3, GROUP)), dma((3, GROUP)),
            dma((SHARE,)), dma((SHARE,)),
            dma((CHUNKS, SHARE)), dma((CHUNKS, SHARE)),
            dma((3, GROUP)), dma((3, GROUP)),
            dma((3, GROUP)), dma((3, GROUP)),
            dma((SHARE,)), dma((SHARE,)),
            dma((16,)), dma((16,)),
            dma((1,)), dma((1,)),
            dma((16,)), dma((16,)),
            pltpu.SemaphoreType.REGULAR, pltpu.SemaphoreType.REGULAR,
        ],
        compiler_params=pltpu.CompilerParams(
            collective_id=0, has_side_effects=True, vmem_limit_bytes=56 << 20
        ),
        cost_estimate=pl.CostEstimate(flops=6 << 30, bytes_accessed=20 << 20, transcendentals=0),
    )(
        *[
            pltpu.with_memory_space_constraint(a, pltpu.HBM)
            for a in (
                tokens, cotangent, *places, pixel_depth, cam_poses.transpose(1, 0, 2), cam_weight, gain, frag_stack
            )
        ],
        *[pltpu.with_memory_space_constraint(a, pltpu.HBM) for a in (frag_block, global_frag, momentum)],
    )
    return pl.pallas_call(
        finish,
        name="finish",
        out_shape=tuple(jax.ShapeDtypeStruct(*one) for one in shapes),
        in_specs=[pl.BlockSpec(memory_space=pltpu.VMEM)] * 5,
        out_specs=(pl.BlockSpec(memory_space=pltpu.HBM),) * 5,
        scratch_shapes=[dma((5,))],
    )(*[pltpu.with_memory_space_constraint(a, pltpu.VMEM) for a in results])


def solution(mesh):
    placed = (
        P(("rep", "fsdp"), None),
        P(("rep", "fsdp"), None),
        P(("rep", "fsdp")),
        P(("rep", "fsdp")),
        P(("rep", "fsdp")),
        P(("rep", "fsdp")),
        P(None, ("rep", "fsdp")),
        P("rep", None, None),
        P("rep", "fsdp", None),
        P("rep", None),
        P("rep", None, "fsdp", None),
        P(),
        P("fsdp", None),
        P("fsdp", None),
    )
    return jax.shard_map(
        shards,
        mesh=mesh,
        in_specs=placed,
        out_specs=(
            P("rep", "fsdp", None),
            P("rep", "fsdp"),
            P("fsdp", None),
            P("fsdp", None),
            P("rep", "fsdp", None),
        ),
        check_vma=False,
    )
```
